32 devices in a mesh: groups: 2 (over y), dp: 16 (over z, x, core).
Axes of the slice: x: 2, y: 2, z: 4, core: 2. Of those that a mesh axis runs over, the one named last changes fastest.
Arguments:
- activations: bfloat16 [64, 2, 64, 4096], P(('groups', 'dp')), parts along dimension 0
- out_grads: bfloat16 [64, 2, 64, 4096], P(('groups', 'dp')), parts along dimension 0
- lengths: int32 [64, 2], P(('groups', 'dp')), parts along dimension 0, may hold values from 16 to 64, as said below
- proj_in: bfloat16 [8192, 64], P(('groups', 'dp')), parts along dimension 0, may hold values from -0.09375 to 0.09375
- proj_out: bfloat16 [8192, 64], P(('groups', 'dp')), parts along dimension 0, may hold values from -0.09375 to 0.09375
- eval_sketches: bfloat16 [128, 4096], P(('groups', 'dp')), parts along dimension 0, may hold values from -0.011962891 to 0.011962891
Outputs:
- scores: float32 [64, 64], P(('groups', 'dp')), parts along dimension 0
The draws below stay inside these ranges and needn't reach their ends.
There are 2 independent parts, one for each index of `groups`. The reference program is written for one: setup_inputs(seed, part) draws one part's arguments, and reference() takes and returns one part's arrays. A program takes and returns all parts, laid end to end along the dimension named above; each array names one. Nothing has to cross between parts.
Inputs may be any that keep to these rules, and one draw needn't show every extreme that they name: `lengths`: some response has exactly 64 live tokens and some exactly 16.
All inputs are finite; a program needn't handle non-finite values.
Results may differ from the reference program's by a relative error of at most 0.0022.
The reference program's roundings to bfloat16 on the way (of `inner`, `outer`, `weight` and `precond`) count: a program that leaves them out, or rounds other values in their place, can miss the bound.
Values may be sent and summed in bfloat16 or wider, within the bound.
No kernel may reach another device: no remote copies, remote signals or barrier semaphores. Data moves between devices by JAX's collectives and lax.ppermute only.
A program may use at most 64 MiB of HBM per device.

```python
import jax
import jax.numpy as jnp
from jax import lax

D = 4096
R = 64
SEQ = 64
PAIRS = 32
EVALS = 64


def rising_field(key):
    pair_scale = 1.0 + 2.0 * jnp.arange(PAIRS, dtype=jnp.float32) / max(PAIRS - 1, 1)
    values = jax.random.normal(key, (PAIRS, 2, SEQ, D), jnp.float32)
    return values * pair_scale[:, None, None, None]


def draw_activations(key, part):
    key = jax.random.fold_in(key, 11)
    return rising_field(key).astype(jnp.bfloat16)


def draw_out_grads(key, part):
    key = jax.random.fold_in(key, 23)
    return rising_field(key).astype(jnp.bfloat16)


def draw_lengths(key, part):
    key = jax.random.fold_in(key, 37)
    drawn = jax.random.randint(key, (PAIRS, 2), SEQ // 4, SEQ + 1, dtype=jnp.int32)
    drawn = drawn.at[0, 0].set(SEQ)
    return drawn.at[0, 1].set(SEQ // 4)


def shard_levels(own_key, shape, pieces, least, top_value):
    def one(dim, blocks):
        steps = jax.random.uniform(jax.random.fold_in(jax.random.fold_in(own_key, 6), dim), (blocks,), jnp.float32, least / len(pieces), top_value / len(pieces))
        return jnp.repeat(jnp.exp(steps), shape[dim] // blocks).reshape((-1,) + (1,) * (len(shape) - dim - 1))

    gain = one(*pieces[0])
    for cut in pieces[1:]:
        gain = gain * one(*cut)
    return gain


def noise(key, extent, spread, reach, cuts=(), held_as=jnp.bfloat16):
    values = spread * jax.random.normal(key, extent, jnp.float32)
    if cuts:
        values = values * shard_levels(key, extent, cuts, -0.22, 0.18)
    return jnp.clip(values, -reach, reach).astype(held_as)


def setup_inputs(seed: int = 0, part: int = 0) -> dict:
    key_of = jax.random.split(jax.random.key(seed), 7)
    part_keys = jax.random.split(jax.random.fold_in(key_of[6], part), 7)
    activations = draw_activations(jax.random.fold_in(jax.random.fold_in(key_of[6], part), 71), part)
    out_grads = draw_out_grads(jax.random.fold_in(jax.random.fold_in(key_of[6], part), 71), part)
    lengths = draw_lengths(jax.random.fold_in(jax.random.fold_in(key_of[6], part), 71), part)
    proj_in = noise(part_keys[3], (D, R), D ** -0.5, 0.09375, ((0, 16),))
    proj_out = noise(part_keys[4], (D, R), D ** -0.5, 0.09375, ((0, 16),))
    eval_sketches = noise(part_keys[5], (EVALS, R * R), 0.002, 0.011962891, ((0, 16),))
    return {"activations": activations, "out_grads": out_grads, "lengths": lengths, "proj_in": proj_in, "proj_out": proj_out, "eval_sketches": eval_sketches}


def factor_solve(matrix_a, matrix_b, stack):
    lower_a = jnp.linalg.cholesky(matrix_a)
    lower_b = jnp.linalg.cholesky(matrix_b)
    count_p = stack.shape[0]
    left = jax.scipy.linalg.cho_solve((lower_a, True), stack.transpose(1, 0, 2).reshape(R, count_p * R))
    left = left.reshape(R, count_p, R).transpose(2, 1, 0).reshape(R, count_p * R)
    right = jax.scipy.linalg.cho_solve((lower_b, True), left)
    return right.reshape(R, count_p, R).transpose(1, 2, 0)

def damped(cov):
    return cov + (0.1 * jnp.trace(cov) / R + 1e-06) * jnp.eye(R, dtype=jnp.float32)

def reference(activations, out_grads, lengths, proj_in, proj_out, eval_sketches):
    inner = jnp.dot(activations.reshape(-1, D).astype(jnp.float32), proj_in.astype(jnp.float32), preferred_element_type=jnp.float32).astype(jnp.bfloat16)
    outer = jnp.dot(out_grads.reshape(-1, D).astype(jnp.float32), proj_out.astype(jnp.float32), preferred_element_type=jnp.float32).astype(jnp.bfloat16)
    position = jnp.arange(SEQ, dtype=jnp.int32)
    live = (position[None, None, :] < lengths[:, :, None]).astype(jnp.float32)
    signs = jnp.array([1.0, -1.0], dtype=jnp.float32)
    weight = (live * signs[None, :, None]).reshape(PAIRS, 2 * SEQ)
    inner_f = inner.astype(jnp.float32).reshape(PAIRS, 2 * SEQ, R)
    outer_f = outer.astype(jnp.float32).reshape(PAIRS, 2 * SEQ, R)
    sketch = jnp.einsum('pto,pti->poi', outer_f * weight[:, :, None], inner_f, precision=lax.Precision.HIGHEST)
    live_rows = live.reshape(PAIRS, 2 * SEQ, 1)
    count = jnp.sum(live)
    cov_in = jnp.einsum('pta,ptb->ab', inner_f * live_rows, inner_f, precision=lax.Precision.HIGHEST) / count
    cov_out = jnp.einsum('pta,ptb->ab', outer_f * live_rows, outer_f, precision=lax.Precision.HIGHEST) / count
    precond = factor_solve(damped(cov_out), damped(cov_in), sketch).astype(jnp.bfloat16).reshape(PAIRS, R * R)
    return lax.dot_general(precond.astype(jnp.float32), eval_sketches.astype(jnp.float32), (((1,), (1,)), ((), ())), preferred_element_type=jnp.float32)
```

```python
import functools

import jax
import jax.numpy as jnp
from jax import lax
from jax.experimental import pallas as pl
from jax.experimental.pallas import tpu as pltpu
from jax.sharding import PartitionSpec as P

F32 = jnp.float32
BF16 = jnp.bfloat16
LANES = 128
SUB = 8
VMEM = pltpu.VMEM
SMEM = pltpu.SMEM


def contract_last(a, b):
    return lax.dot_general(a, b, (((1,), (1,)), ((), ())), preferred_element_type=F32)


def contract_first(a, b):
    return lax.dot_general(a, b, (((0,), (0,)), ((), ())), preferred_element_type=F32)


def project_kernel(
    core_ref, lengths_ref, act_ref, grad_ref, own_ref, other_ref, keep_ref, send_ref, sketch_ref
):
    place, core = core_ref[0], core_ref[1]
    blocks, both_ranks, chunk = own_ref.shape
    rank = both_ranks // 2
    pairs, _ = lengths_ref.shape
    rows = act_ref.shape[0]
    seq = rows // (2 * pairs)

    def project(x_ref, first):
        total = jnp.zeros((rows, rank), F32)
        for g in range(blocks):
            for ref, at in ((own_ref, place), (other_ref, 1 - place)):
                start = pl.multiple_of((2 * g + at) * chunk, chunk)
                total += contract_last(
                    x_ref[:, pl.ds(start, chunk)], ref[g, first : first + rank, :]
                )
        return total

    token = lax.broadcasted_iota(jnp.int32, (seq, rank), 0)

    def masked(total):
        parts = []
        for s in range(2 * pairs):
            live = token < lengths_ref[s // 2, s % 2]
            parts.append(jnp.where(live, total[s * seq : (s + 1) * seq], 0.0))
        return parts

    inner_parts = masked(project(act_ref, 0))
    outer_parts = masked(project(grad_ref, rank))
    inner = jnp.concatenate(inner_parts, 0).astype(BF16)
    outer = jnp.concatenate(outer_parts, 0).astype(BF16)
    signed = jnp.concatenate(
        [-part if s % 2 else part for s, part in enumerate(outer_parts)], 0
    ).astype(BF16)
    sketches = []
    for p in range(pairs):
        own_rows = slice(2 * p * seq, 2 * (p + 1) * seq)
        sketches.append(contract_first(signed[own_rows], inner[own_rows]))
    sketch_ref[...] = jnp.concatenate(sketches, 1)

    count = lengths_ref[0, 0]
    for s in range(1, 2 * pairs):
        count += lengths_ref[s // 2, s % 2]
    half = rank // 2
    row = lax.broadcasted_iota(jnp.int32, (half, 2 * rank), 0)
    lane = lax.broadcasted_iota(jnp.int32, (half, 2 * rank), 1)
    slot = (row == 0) & (lane == rank)

    def packed(rows_of):
        cov = contract_first(rows_of, rows_of)
        wide = jnp.concatenate([cov[:half], cov[half:]], 1)
        return jnp.where(slot, count.astype(F32), wide)

    cov_in = packed(inner)
    cov_out = packed(outer)
    first_core = core == 0
    keep_ref[...] = jnp.where(first_core, cov_in, cov_out)
    send_ref[...] = jnp.where(first_core, cov_out, cov_in)


def gauss_jordan(tiles, width, group):
    count = len(tiles)
    sub = lax.broadcasted_iota(jnp.int32, tiles[0].shape, 0)
    shape = tiles[0].shape

    def spread_row(tile, j):
        return jnp.broadcast_to(tile[j : j + 1, :], shape)

    for start in range(0, width, group):
        columns = [
            [jnp.broadcast_to(tile[:, k : k + 1], shape) for tile in tiles]
            for k in range(start, start + group)
        ]
        for step in range(group):
            home, j = divmod(start + step, SUB)
            column = columns[step]
            inverse = 1.0 / spread_row(column[home], j)

            def eliminate(block):
                scaled = spread_row(block[home], j) * inverse
                result = [block[g] - column[g] * scaled for g in range(count)]
                result[home] = jnp.where(sub == j, scaled, result[home])
                return result

            for later in range(step + 1, group):
                columns[later] = eliminate(columns[later])
            tiles = eliminate(tiles)
    return tiles


def invert_kernel(blocks_ref, inverse_ref):
    _, half, wide = blocks_ref.shape
    rank = 2 * half
    total = jnp.sum(blocks_ref[...], axis=0)
    row = lax.broadcasted_iota(jnp.int32, (half, wide), 0)
    lane = lax.broadcasted_iota(jnp.int32, (half, wide), 1)
    slot = (row == 0) & (lane == rank)
    mirror = (row == 0) & (lane == half)
    diagonal = (lane == row) | (lane == row + rank + half)

    def pick(mask):
        return jnp.sum(jnp.where(mask, total, 0.0), axis=(0, 1), keepdims=True)

    count = pick(slot)
    damp = 0.1 * (pick(diagonal) / count) / rank + 1e-06
    total = jnp.where(slot, pick(mirror), total)
    matrix = total / count + jnp.where(diagonal, damp, 0.0)
    left = jnp.concatenate([matrix[:, :rank], matrix[:, rank:]], 0)
    row = lax.broadcasted_iota(jnp.int32, (rank, rank), 0)
    lane = lax.broadcasted_iota(jnp.int32, (rank, rank), 1)
    both = jnp.concatenate([left, jnp.where(row == lane, 1.0, 0.0)], 1)
    tiles = [both[g * SUB : (g + 1) * SUB] for g in range(rank // SUB)]
    tiles = gauss_jordan(tiles, rank, 4)
    inverse_ref[...] = jnp.concatenate([tile[:, rank:] for tile in tiles], 0)


def precond_kernel(core_ref, own_ref, other_ref, sketch_ref, precond_ref):
    first_core = core_ref[0] == 0
    own = own_ref[...]
    other = other_ref[...]
    inverse_in = jnp.where(first_core, own, other)
    inverse_out = jnp.where(first_core, other, own)
    rank = own.shape[0]
    left = jnp.dot(
        inverse_out, sketch_ref[...], precision=lax.Precision.HIGHEST, preferred_element_type=F32
    )
    for p in range(precond_ref.shape[0]):
        right = jnp.dot(
            left[:, p * rank : (p + 1) * rank],
            inverse_in,
            precision=lax.Precision.HIGHEST,
            preferred_element_type=F32,
        )
        precond_ref[p] = right.astype(BF16)


def whole(space=VMEM):
    return pl.BlockSpec(memory_space=space)


def on_device(devices, activations, out_grads, lengths, proj_in, proj_out, eval_sketches):
    pairs, _, seq, depth = activations.shape
    rank = proj_in.shape[1]
    chips = devices // 2
    same_core = [[2 * chip + core for chip in range(chips)] for core in range(2)]
    swap = [(d, d ^ 1) for d in range(devices)]
    place = lax.axis_index("dp")
    core = (place % 2).astype(jnp.int32).reshape(1)

    def to_all_chips(block):
        copies = jnp.broadcast_to(block[None], (chips,) + block.shape)
        return lax.all_to_all(copies, "dp", 0, 0, axis_index_groups=same_core)

    every_eval = lax.all_gather(eval_sketches, ("groups", "dp"), axis=0, tiled=True)
    evals = every_eval.shape[0] // lax.axis_size("groups")
    every_eval = lax.dynamic_slice_in_dim(every_eval, lax.axis_index("groups") * evals, evals, 0)

    mine = jnp.concatenate([proj_in, proj_out], 1).T
    own = to_all_chips(mine)
    other = lax.ppermute(own, "dp", swap)
    slot_core = core
    local = mine.shape[1]
    if local % LANES:
        stacked = jnp.where(place % 2 == 0, jnp.stack([own, other], 1), jnp.stack([other, own], 1))
        full = stacked.transpose(2, 0, 1, 3).reshape(2 * rank, depth)
        split = full.reshape(2 * rank, -1, 2, 2 * LANES).transpose(1, 2, 0, 3)
        own, other = split[:, 0], split[:, 1]
        slot_core = jnp.zeros((1,), jnp.int32)

    rows = 2 * pairs * seq
    half = rank // 2
    keep, send, sketch = pl.pallas_call(
        project_kernel,
        out_shape=(
            jax.ShapeDtypeStruct((half, 2 * rank), F32),
            jax.ShapeDtypeStruct((half, 2 * rank), F32),
            jax.ShapeDtypeStruct((rank, pairs * rank), F32),
        ),
        in_specs=[whole(SMEM), whole(SMEM)] + [whole()] * 4,
        out_specs=(whole(), whole(), whole()),
        name="project",
    )(
        jnp.concatenate([slot_core, core]),
        lengths,
        activations.reshape(rows, depth),
        out_grads.reshape(rows, depth),
        own,
        other,
    )
    chip_sum = keep + lax.ppermute(send, "dp", swap)
    blocks = to_all_chips(chip_sum)
    inverse = pl.pallas_call(
        invert_kernel,
        out_shape=jax.ShapeDtypeStruct((rank, rank), F32),
        in_specs=[whole()],
        out_specs=whole(),
        name="invert",
    )(blocks)
    other_inverse = lax.ppermute(inverse, "dp", swap)
    precond = pl.pallas_call(
        precond_kernel,
        out_shape=jax.ShapeDtypeStruct((pairs, rank, rank), BF16),
        in_specs=[whole(SMEM)] + [whole()] * 3,
        out_specs=whole(),
        name="precond",
    )(core, inverse, other_inverse, sketch)
    return contract_last(precond.reshape(pairs, rank * rank), every_eval)


def solution(mesh):
    in_specs = (
        P(("groups", "dp"), None, None, None),
        P(("groups", "dp"), None, None, None),
        P(("groups", "dp"), None),
        P(("groups", "dp"), None),
        P(("groups", "dp"), None),
        P(("groups", "dp"), None),
    )
    out_specs = P(("groups", "dp"), None)
    return jax.shard_map(
        functools.partial(on_device, mesh.shape["dp"]),
        mesh=mesh,
        in_specs=in_specs,
        out_specs=out_specs,
        check_vma=False,
    )
```

```python
import functools

import jax
import jax.numpy as jnp
from jax import lax
from jax.experimental import pallas as pl
from jax.experimental.pallas import tpu as pltpu
from jax.sharding import PartitionSpec as P

F32 = jnp.float32
BF16 = jnp.bfloat16
LANES = 128
SUB = 8
VMEM = pltpu.VMEM
SMEM = pltpu.SMEM


def contract_last(a, b):
    return lax.dot_general(a, b, (((1,), (1,)), ((), ())), preferred_element_type=F32)


def contract_first(a, b):
    return lax.dot_general(a, b, (((0,), (0,)), ((), ())), preferred_element_type=F32)


def project_kernel(
    core_ref, lengths_ref, act_ref, grad_ref, own_ref, other_ref, keep_ref, send_ref, sketch_ref
):
    place, core = core_ref[0], core_ref[1]
    blocks, both_ranks, chunk = own_ref.shape
    rank = both_ranks // 2
    pairs, _ = lengths_ref.shape
    rows = act_ref.shape[0]
    seq = rows // (2 * pairs)

    def project(x_ref, first):
        total = jnp.zeros((rows, rank), F32)
        for g in range(blocks):
            for ref, at in ((own_ref, place), (other_ref, 1 - place)):
                start = pl.multiple_of((2 * g + at) * chunk, chunk)
                total += contract_last(
                    x_ref[:, pl.ds(start, chunk)], ref[g, first : first + rank, :]
                )
        return total

    token = lax.broadcasted_iota(jnp.int32, (seq, rank), 0)

    def masked(total):
        parts = []
        for s in range(2 * pairs):
            live = token < lengths_ref[s // 2, s % 2]
            parts.append(jnp.where(live, total[s * seq : (s + 1) * seq], 0.0))
        return parts

    inner_parts = masked(project(act_ref, 0))
    outer_parts = masked(project(grad_ref, rank))
    inner = jnp.concatenate(inner_parts, 0).astype(BF16)
    outer = jnp.concatenate(outer_parts, 0).astype(BF16)
    signed = jnp.concatenate(
        [-part if s % 2 else part for s, part in enumerate(outer_parts)], 0
    ).astype(BF16)
    sketches = []
    for p in range(pairs):
        own_rows = slice(2 * p * seq, 2 * (p + 1) * seq)
        sketches.append(contract_first(signed[own_rows], inner[own_rows]))
    sketch_ref[...] = jnp.concatenate(sketches, 1)

    count = lengths_ref[0, 0]
    for s in range(1, 2 * pairs):
        count += lengths_ref[s // 2, s % 2]
    half = rank // 2
    row = lax.broadcasted_iota(jnp.int32, (half, 2 * rank), 0)
    lane = lax.broadcasted_iota(jnp.int32, (half, 2 * rank), 1)
    slot = (row == 0) & (lane == rank)

    def packed(rows_of):
        cov = contract_first(rows_of, rows_of)
        wide = jnp.concatenate([cov[:half], cov[half:]], 1)
        return jnp.where(slot, count.astype(F32), wide)

    cov_in = packed(inner)
    cov_out = packed(outer)
    first_core = core == 0
    keep_ref[...] = jnp.where(first_core, cov_in, cov_out)
    send_ref[...] = jnp.where(first_core, cov_out, cov_in)


def gauss_jordan(tiles, width, group):
    count = len(tiles)
    sub = lax.broadcasted_iota(jnp.int32, tiles[0].shape, 0)
    shape = tiles[0].shape

    def spread_row(tile, j):
        return jnp.broadcast_to(tile[j : j + 1, :], shape)

    for start in range(0, width, group):
        columns = [
            [jnp.broadcast_to(tile[:, k : k + 1], shape) for tile in tiles]
            for k in range(start, start + group)
        ]
        for step in range(group):
            home, j = divmod(start + step, SUB)
            column = columns[step]
            inverse = 1.0 / spread_row(column[home], j)

            def eliminate(block):
                scaled = spread_row(block[home], j) * inverse
                result = [block[g] - column[g] * scaled for g in range(count)]
                result[home] = jnp.where(sub == j, scaled, result[home])
                return result

            for later in range(step + 1, group):
                columns[later] = eliminate(columns[later])
            tiles = eliminate(tiles)
    return tiles


def invert_kernel(blocks_ref, inverse_ref):
    _, half, wide = blocks_ref.shape
    rank = 2 * half
    total = jnp.sum(blocks_ref[...], axis=0)
    row = lax.broadcasted_iota(jnp.int32, (half, wide), 0)
    lane = lax.broadcasted_iota(jnp.int32, (half, wide), 1)
    slot = (row == 0) & (lane == rank)
    mirror = (row == 0) & (lane == half)
    diagonal = (lane == row) | (lane == row + rank + half)

    def pick(mask):
        return jnp.sum(jnp.where(mask, total, 0.0), axis=(0, 1), keepdims=True)

    count = pick(slot)
    damp = 0.1 * (pick(diagonal) / count) / rank + 1e-06
    total = jnp.where(slot, pick(mirror), total)
    matrix = total / count + jnp.where(diagonal, damp, 0.0)
    left = jnp.concatenate([matrix[:, :rank], matrix[:, rank:]], 0)
    row = lax.broadcasted_iota(jnp.int32, (rank, rank), 0)
    lane = lax.broadcasted_iota(jnp.int32, (rank, rank), 1)
    both = jnp.concatenate([left, jnp.where(row == lane, 1.0, 0.0)], 1)
    tiles = [both[g * SUB : (g + 1) * SUB] for g in range(rank // SUB)]
    tiles = gauss_jordan(tiles, rank, 4)
    inverse_ref[...] = jnp.concatenate([tile[:, rank:] for tile in tiles], 0)


def precond_kernel(core_ref, own_ref, other_ref, sketch_ref, precond_ref):
    first_core = core_ref[0] == 0
    own = own_ref[...]
    other = other_ref[...]
    inverse_in = jnp.where(first_core, own, other)
    inverse_out = jnp.where(first_core, other, own)
    rank = own.shape[0]
    left = jnp.dot(
        inverse_out, sketch_ref[...], precision=lax.Precision.HIGHEST, preferred_element_type=F32
    )
    for p in range(precond_ref.shape[0]):
        right = jnp.dot(
            left[:, p * rank : (p + 1) * rank],
            inverse_in,
            precision=lax.Precision.HIGHEST,
            preferred_element_type=F32,
        )
        precond_ref[p] = right.astype(BF16)


def params(mebibytes):
    return pltpu.CompilerParams(vmem_limit_bytes=mebibytes * 2**20)


def whole(space=VMEM):
    return pl.BlockSpec(memory_space=space)


def on_device(devices, activations, out_grads, lengths, proj_in, proj_out, eval_sketches):
    pairs, _, seq, depth = activations.shape
    rank = proj_in.shape[1]
    chips = devices // 2
    same_core = [[2 * chip + core for chip in range(chips)] for core in range(2)]
    swap = [(d, d ^ 1) for d in range(devices)]
    place = lax.axis_index("dp")
    core = (place % 2).astype(jnp.int32).reshape(1)

    def to_all_chips(block):
        copies = jnp.broadcast_to(block[None], (chips,) + block.shape)
        return lax.all_to_all(copies, "dp", 0, 0, axis_index_groups=same_core)

    own_evals = to_all_chips(eval_sketches)
    other_evals = lax.ppermute(own_evals, "dp", swap)

    mine = jnp.concatenate([proj_in, proj_out], 1).T
    own = to_all_chips(mine)
    other = lax.ppermute(own, "dp", swap)
    slot_core = core
    local = mine.shape[1]
    if local % LANES:
        stacked = jnp.where(place % 2 == 0, jnp.stack([own, other], 1), jnp.stack([other, own], 1))
        full = stacked.transpose(2, 0, 1, 3).reshape(2 * rank, depth)
        split = full.reshape(2 * rank, -1, 2, 2 * LANES).transpose(1, 2, 0, 3)
        own, other = split[:, 0], split[:, 1]
        slot_core = jnp.zeros((1,), jnp.int32)

    rows = 2 * pairs * seq
    half = rank // 2
    keep, send, sketch = pl.pallas_call(
        project_kernel,
        out_shape=(
            jax.ShapeDtypeStruct((half, 2 * rank), F32),
            jax.ShapeDtypeStruct((half, 2 * rank), F32),
            jax.ShapeDtypeStruct((rank, pairs * rank), F32),
        ),
        in_specs=[whole(SMEM), whole(SMEM)] + [whole()] * 4,
        out_specs=(whole(), whole(), whole()),
        compiler_params=params(24),
        cost_estimate=pl.CostEstimate(flops=4 * rows * depth * rank, bytes_accessed=6 * rows * depth, transcendentals=0),
        name="project",
    )(
        jnp.concatenate([slot_core, core]),
        lengths,
        activations.reshape(rows, depth),
        out_grads.reshape(rows, depth),
        own,
        other,
    )
    chip_sum = keep + lax.ppermute(send, "dp", swap)
    blocks = to_all_chips(chip_sum)
    inverse = pl.pallas_call(
        invert_kernel,
        out_shape=jax.ShapeDtypeStruct((rank, rank), F32),
        in_specs=[whole()],
        out_specs=whole(),
        compiler_params=params(4),
        cost_estimate=pl.CostEstimate(flops=10**9, bytes_accessed=2**24, transcendentals=0),
        name="invert",
    )(blocks)
    other_inverse = lax.ppermute(inverse, "dp", swap)
    precond = pl.pallas_call(
        precond_kernel,
        out_shape=jax.ShapeDtypeStruct((pairs, rank, rank), BF16),
        in_specs=[whole(SMEM)] + [whole()] * 3,
        out_specs=whole(),
        compiler_params=params(4),
        name="precond",
    )(core, inverse, other_inverse, sketch)
    in_order = jnp.where(place % 2 == 0, jnp.stack([own_evals, other_evals], 1), jnp.stack([other_evals, own_evals], 1))
    return contract_last(precond.reshape(pairs, rank * rank), in_order.reshape(-1, rank * rank))


def solution(mesh):
    in_specs = (
        P(("groups", "dp"), None, None, None),
        P(("groups", "dp"), None, None, None),
        P(("groups", "dp"), None),
        P(("groups", "dp"), None),
        P(("groups", "dp"), None),
        P(("groups", "dp"), None),
    )
    out_specs = P(("groups", "dp"), None)
    return jax.shard_map(
        functools.partial(on_device, mesh.shape["dp"]),
        mesh=mesh,
        in_specs=in_specs,
        out_specs=out_specs,
        check_vma=False,
    )
```

```python
import functools

import jax
import jax.numpy as jnp
from jax import lax
from jax.experimental import pallas as pl
from jax.experimental.pallas import tpu as pltpu
from jax.sharding import PartitionSpec as P

F32 = jnp.float32
BF16 = jnp.bfloat16
LANES = 128
SUB = 8
VMEM = pltpu.VMEM
SMEM = pltpu.SMEM


def contract_last(a, b):
    return lax.dot_general(a, b, (((1,), (1,)), ((), ())), preferred_element_type=F32)


def contract_first(a, b):
    return lax.dot_general(a, b, (((0,), (0,)), ((), ())), preferred_element_type=F32)


def packed_symmetric(matrix):
    half = matrix.shape[0] // 2
    quarter = half // 4
    corners = (matrix[:half, :half], matrix[:half, half:], matrix[half:, half:])
    return jnp.concatenate(
        [
            jnp.concatenate([c[quarter * j : quarter * (j + 1)] for j in range(4)], 1)
            for c in corners
        ],
        0,
    )


def unpacked_symmetric(packed):
    quarter, wide = packed.shape[0] // 3, packed.shape[1]
    half = wide // 4
    corners = []
    for c in range(3):
        rows = packed[c * quarter : (c + 1) * quarter]
        corners.append(
            jnp.concatenate([rows[:, half * j : half * (j + 1)] for j in range(4)], 0)
        )
    first, cross, last = corners
    return jnp.concatenate(
        [jnp.concatenate([first, cross], 1), jnp.concatenate([cross.T, last], 1)], 0
    )


def packed_places(shape):
    quarter = shape[0] // 3
    half = shape[1] // 4
    row = lax.broadcasted_iota(jnp.int32, shape, 0)
    lane = lax.broadcasted_iota(jnp.int32, shape, 1)
    slot = (row == 0) & (lane == half)
    mirror = (row == 0) & (lane == quarter)
    diagonal = (lane % half == (lane // half) * quarter + row % quarter) & (
        (row < quarter) | (row >= 2 * quarter)
    )
    return slot, mirror, diagonal


def stage_kernel(*refs):
    count = len(refs) // 2
    arrived = refs[-1]
    copies = [
        pltpu.make_async_copy(refs[i], refs[count + i], arrived.at[i]) for i in range(count)
    ]
    for copy in copies:
        copy.start()
    for copy in copies:
        copy.wait()


def staged(*arrays):
    count = len(arrays)
    return pl.pallas_call(
        stage_kernel,
        out_shape=tuple(jax.ShapeDtypeStruct(a.shape, a.dtype) for a in arrays),
        in_specs=[whole(pl.ANY)] * count,
        out_specs=(whole(pl.ANY),) * count,
        scratch_shapes=[pltpu.SemaphoreType.DMA((count,))],
        compiler_params=params(1),
        cost_estimate=pl.CostEstimate(flops=0, bytes_accessed=2**22, transcendentals=0),
        name="stage",
    )(*arrays)


def project_kernel(
    numbers_ref,
    lengths_ref,
    act_ref,
    grad_ref,
    own_ref,
    other_ref,
    evals_ref,
    keep_ref,
    send_ref,
    sketch_ref,
    same_evals_ref,
):
    same_evals_ref[...] = evals_ref[...]
    place, core = numbers_ref[0], numbers_ref[1]
    sequences = 2 * lengths_ref.shape[0]
    length_of = [lengths_ref[s // 2, s % 2] for s in range(sequences)]
    blocks, both_ranks, chunk = own_ref.shape
    rank = both_ranks // 2
    pairs = sequences // 2
    rows, depth = act_ref.shape
    seq = rows // sequences
    def project(x_ref, first):
        total = jnp.zeros((rows, rank), F32)
        for g in range(blocks):
            for ref, at in ((own_ref, place), (other_ref, 1 - place)):
                start = pl.multiple_of((2 * g + at) * chunk, chunk)
                total += contract_last(
                    x_ref[:, pl.ds(start, chunk)], ref[g, first : first + rank, :]
                )
        return total

    token = lax.broadcasted_iota(jnp.int32, (seq, rank), 0)

    def masked(total):
        kept = []
        for s in range(sequences):
            live = token < length_of[s]
            kept.append(jnp.where(live, total[s * seq : (s + 1) * seq], 0.0))
        return kept

    count = functools.reduce(lambda a, b: a + b, length_of)
    slot, _, _ = packed_places(keep_ref.shape)

    def factor(rows_of):
        packed = packed_symmetric(contract_first(rows_of, rows_of))
        return jnp.where(slot, count.astype(F32), packed)

    inner = jnp.concatenate(masked(project(act_ref, 0)), 0).astype(BF16)
    outer_parts = masked(project(grad_ref, rank))
    factor_out = factor(jnp.concatenate(outer_parts, 0).astype(BF16))
    factor_in = factor(inner)
    first_core = core == 0
    keep_ref[...] = jnp.where(first_core, factor_in, factor_out)
    send_ref[...] = jnp.where(first_core, factor_out, factor_in)
    signed = jnp.concatenate(
        [-part if s % 2 else part for s, part in enumerate(outer_parts)], 0
    ).astype(BF16)
    sketches = []
    for p in range(pairs):
        own_rows = slice(2 * p * seq, 2 * (p + 1) * seq)
        sketches.append(contract_first(signed[own_rows], inner[own_rows]))
    sketch_ref[...] = jnp.concatenate(sketches, 1)


def gauss_jordan(tiles, width, group):
    count = len(tiles)
    sub = lax.broadcasted_iota(jnp.int32, tiles[0].shape, 0)
    shape = tiles[0].shape

    def spread_row(tile, j):
        return jnp.broadcast_to(tile[j : j + 1, :], shape)

    for start in range(0, width, group):
        columns = [
            [jnp.broadcast_to(tile[:, k : k + 1], shape) for tile in tiles]
            for k in range(start, start + group)
        ]
        for step in range(group):
            home, j = divmod(start + step, SUB)
            column = columns[step]
            inverse = 1.0 / spread_row(column[home], j)

            def eliminate(block):
                scaled = spread_row(block[home], j) * inverse
                result = [block[g] - column[g] * scaled for g in range(count)]
                result[home] = jnp.where(sub == j, scaled, result[home])
                return result

            for later in range(step + 1, group):
                columns[later] = eliminate(columns[later])
            tiles = eliminate(tiles)
    return tiles


def invert_kernel(blocks_ref, inverse_ref):
    rank = inverse_ref.shape[0]
    total = jnp.sum(blocks_ref[...], axis=0)
    slot, mirror, diagonal = packed_places(total.shape)

    def pick(mask):
        return jnp.sum(jnp.where(mask, total, 0.0), axis=(0, 1), keepdims=True)

    count = pick(slot)
    damp = 0.1 * (pick(diagonal) / count) / rank + 1e-06
    total = jnp.where(slot, pick(mirror), total)
    matrix = unpacked_symmetric(total / count + jnp.where(diagonal, damp, 0.0))
    row = lax.broadcasted_iota(jnp.int32, (rank, rank), 0)
    lane = lax.broadcasted_iota(jnp.int32, (rank, rank), 1)
    both = jnp.concatenate([matrix, jnp.where(row == lane, 1.0, 0.0)], 1)
    tiles = [both[g * SUB : (g + 1) * SUB] for g in range(rank // SUB)]
    tiles = gauss_jordan(tiles, rank, SUB)
    inverse_ref[...] = jnp.concatenate([tile[:, rank:] for tile in tiles], 0)


def exact_dot(a, b):
    return jnp.dot(a, b, precision=lax.Precision.HIGHEST, preferred_element_type=F32)


def score_kernel(
    bits, place_ref, own_ref, other_ref, sketch_ref, near_ref, far_ref, scores_ref, rows_ref
):
    place = place_ref[0]
    first_core = place % 2 == 0
    own = own_ref[...]
    other = other_ref[...]
    inverse_in = jnp.where(first_core, own, other)
    inverse_out = jnp.where(first_core, other, own)
    rank = own.shape[0]
    pairs, evals = scores_ref.shape
    left = exact_dot(inverse_out, sketch_ref[...])
    for p in range(pairs):
        rows_ref[p * rank : (p + 1) * rank, :] = exact_dot(
            left[:, p * rank : (p + 1) * rank], inverse_in
        )
    fold = 2 * LANES // rank
    steps = rank // fold
    precond = jnp.concatenate(
        [rows_ref[pl.ds(j, pairs * steps, stride=fold), :] for j in range(fold)], 1
    ).astype(BF16)
    row = lax.broadcasted_iota(jnp.int32, (pairs * steps, evals), 0) % steps
    total = jnp.zeros((pairs * steps, evals), F32)
    for g in range(steps):
        lanes = slice(g * fold * rank, (g + 1) * fold * rank)
        sketches = jnp.concatenate([near_ref[:, lanes], far_ref[:, lanes]], 0)
        total += jnp.where(row == g, contract_last(precond, sketches), 0.0)
    scores = jnp.concatenate(
        [jnp.sum(total[p * steps : (p + 1) * steps], 0, keepdims=True) for p in range(pairs)], 0
    )
    held = evals >> len(bits)
    column = lax.broadcasted_iota(jnp.int32, (evals, evals), 0)
    block = column // held
    source = jnp.full((evals, evals), place, jnp.int32)
    for i, bit in enumerate(bits):
        source = source ^ (((block >> i) & 1) * bit)
    target = source * held + column % held
    order = jnp.where(target == lax.broadcasted_iota(jnp.int32, (evals, evals), 1), 1.0, 0.0)
    scores_ref[...] = exact_dot(scores, order)


def params(mebibytes):
    return pltpu.CompilerParams(vmem_limit_bytes=mebibytes * 2**20)


def whole(space=VMEM):
    return pl.BlockSpec(memory_space=space)


def on_device(devices, activations, out_grads, lengths, proj_in, proj_out, eval_sketches):
    pairs, _, seq, depth = activations.shape
    rank = proj_in.shape[1]
    chips = devices // 2
    same_core = [[2 * chip + core for chip in range(chips)] for core in range(2)]
    place = lax.axis_index("dp").astype(jnp.int32).reshape(1)
    core = place % 2
    bits = [2**i for i in range(2, devices.bit_length() - 1)] + [2, 1]
    mid, late = bits[:-2], bits[-2]

    def swap(block, bit):
        return lax.ppermute(block, "dp", [(d, d ^ bit) for d in range(devices)])

    def copies_of(block):
        return jnp.broadcast_to(block[None], (chips,) + block.shape)

    def to_all_chips(copies):
        return lax.all_to_all(copies, "dp", 0, 0, axis_index_groups=same_core)

    def doubled(block, bit):
        return jnp.concatenate([block, swap(block, bit)], 0)

    rows = 2 * pairs * seq
    flat_in, flat_out, near = staged(
        activations.reshape(rows, depth), out_grads.reshape(rows, depth), eval_sketches
    )
    near = doubled(near, mid[0])
    mine = jnp.concatenate([proj_in, proj_out], 1).T
    own = to_all_chips(copies_of(mine))
    own, near = lax.optimization_barrier((own, near))
    other = swap(own, 1)
    for bit in mid[1:-1]:
        near = doubled(near, bit)
    arriving = swap(near, mid[-1])
    slot_core = core
    local = mine.shape[1]
    if local % LANES:
        stacked = jnp.where(
            core[0] == 0, jnp.stack([own, other], 1), jnp.stack([other, own], 1)
        )
        full = stacked.transpose(2, 0, 1, 3).reshape(2 * rank, depth)
        split = full.reshape(2 * rank, -1, 2, 2 * LANES).transpose(1, 2, 0, 3)
        own, other = split[:, 0], split[:, 1]
        slot_core = jnp.zeros((1,), jnp.int32)

    packed = jax.ShapeDtypeStruct((3 * rank // 8, 2 * rank), F32)
    keep, send, sketch, near = pl.pallas_call(
        project_kernel,
        out_shape=(
            packed,
            packed,
            jax.ShapeDtypeStruct((rank, pairs * rank), F32),
            jax.ShapeDtypeStruct(near.shape, near.dtype),
        ),
        in_specs=[whole(SMEM)] * 2 + [whole()] * 5,
        out_specs=(whole(),) * 4,
        compiler_params=params(24),
        cost_estimate=pl.CostEstimate(
            flops=4 * rows * depth * rank, bytes_accessed=6 * rows * depth, transcendentals=0
        ),
        name="project",
    )(
        jnp.concatenate([slot_core, core]),
        lengths,
        flat_in,
        flat_out,
        own,
        other,
        near,
    )
    sums = copies_of(keep + swap(send, 1))
    blocks = to_all_chips(sums)
    near = doubled(jnp.concatenate([near, arriving], 0), late)
    far = swap(near, 1)
    inverse = pl.pallas_call(
        invert_kernel,
        out_shape=jax.ShapeDtypeStruct((rank, rank), F32),
        in_specs=[whole()],
        out_specs=whole(),
        compiler_params=params(4),
        cost_estimate=pl.CostEstimate(flops=10**9, bytes_accessed=2**24, transcendentals=0),
        name="invert",
    )(blocks)
    other_inverse = swap(inverse, 1)
    evals = 2 * near.shape[0]
    return pl.pallas_call(
        functools.partial(score_kernel, bits),
        out_shape=jax.ShapeDtypeStruct((pairs, evals), F32),
        in_specs=[whole(SMEM)] + [whole()] * 5,
        out_specs=whole(),
        scratch_shapes=[pltpu.VMEM((pairs * rank, rank), F32)],
        compiler_params=params(4 + 6 * evals * rank * rank // 2**20),
        name="score",
    )(place, inverse, other_inverse, sketch, near, far)


def solution(mesh):
    in_specs = (
        P(("groups", "dp"), None, None, None),
        P(("groups", "dp"), None, None, None),
        P(("groups", "dp"), None),
        P(("groups", "dp"), None),
        P(("groups", "dp"), None),
        P(("groups", "dp"), None),
    )
    out_specs = P(("groups", "dp"), None)
    return jax.shard_map(
        functools.partial(on_device, mesh.shape["dp"]),
        mesh=mesh,
        in_specs=in_specs,
        out_specs=out_specs,
        check_vma=False,
    )
```

```python
import functools

import jax
import jax.numpy as jnp
from jax import lax
from jax.experimental import pallas as pl
from jax.experimental.pallas import tpu as pltpu
from jax.sharding import PartitionSpec as P

F32 = jnp.float32
BF16 = jnp.bfloat16
LANES = 128
SUB = 8
VMEM = pltpu.VMEM
SMEM = pltpu.SMEM


def contract_last(a, b):
    return lax.dot_general(a, b, (((1,), (1,)), ((), ())), preferred_element_type=F32)


def contract_first(a, b):
    return lax.dot_general(a, b, (((0,), (0,)), ((), ())), preferred_element_type=F32)


def packed_symmetric(matrix):
    half = matrix.shape[0] // 2
    quarter = half // 4
    corners = (matrix[:half, :half], matrix[:half, half:], matrix[half:, half:])
    return jnp.concatenate(
        [
            jnp.concatenate([c[quarter * j : quarter * (j + 1)] for j in range(4)], 1)
            for c in corners
        ],
        0,
    )


def unpacked_symmetric(packed):
    quarter, wide = packed.shape[0] // 3, packed.shape[1]
    half = wide // 4
    corners = []
    for c in range(3):
        rows = packed[c * quarter : (c + 1) * quarter]
        corners.append(
            jnp.concatenate([rows[:, half * j : half * (j + 1)] for j in range(4)], 0)
        )
    first, cross, last = corners
    return jnp.concatenate(
        [jnp.concatenate([first, cross], 1), jnp.concatenate([cross.T, last], 1)], 0
    )


def packed_places(shape):
    quarter = shape[0] // 3
    half = shape[1] // 4
    row = lax.broadcasted_iota(jnp.int32, shape, 0)
    lane = lax.broadcasted_iota(jnp.int32, shape, 1)
    slot = (row == 0) & (lane == half)
    mirror = (row == 0) & (lane == quarter)
    diagonal = (lane % half == (lane // half) * quarter + row % quarter) & (
        (row < quarter) | (row >= 2 * quarter)
    )
    return slot, mirror, diagonal


def projected(x_ref, blocks_ref, first, rank, place, total):
    blocks, _, chunk = blocks_ref.shape
    for g in range(blocks):
        start = pl.multiple_of((2 * g + place) * chunk, chunk)
        total += contract_last(
            x_ref[:, pl.ds(start, chunk)], blocks_ref[g, first : first + rank, :]
        )
    return total


def own_place(split_cores):
    return lax.axis_index("dp") % 2 if split_cores else 0


def first_half_kernel(split_cores, first, x_ref, own_ref, total_ref):
    total_ref[...] = projected(
        x_ref,
        own_ref,
        first,
        total_ref.shape[1],
        own_place(split_cores),
        jnp.zeros(total_ref.shape, F32),
    )


def second_half_kernel(
    split_cores,
    lengths_ref,
    act_ref,
    grad_ref,
    other_ref,
    half_in_ref,
    half_out_ref,
    keep_ref,
    send_ref,
    sketch_ref,
):
    place = 1 - own_place(split_cores)
    sequences = 2 * lengths_ref.shape[0]
    length_of = [lengths_ref[s // 2, s % 2] for s in range(sequences)]
    pairs = sequences // 2
    rows, rank = half_in_ref.shape
    seq = rows // sequences
    token = lax.broadcasted_iota(jnp.int32, (seq, rank), 0)

    def masked(total):
        kept = []
        for s in range(sequences):
            live = token < length_of[s]
            kept.append(jnp.where(live, total[s * seq : (s + 1) * seq], 0.0))
        return kept

    count = functools.reduce(lambda a, b: a + b, length_of)
    slot, _, _ = packed_places(keep_ref.shape)

    def factor(rows_of):
        packed = packed_symmetric(contract_first(rows_of, rows_of))
        return jnp.where(slot, count.astype(F32), packed)

    total_in = projected(act_ref, other_ref, 0, rank, place, half_in_ref[...])
    total_out = projected(grad_ref, other_ref, rank, rank, place, half_out_ref[...])
    inner = jnp.concatenate(masked(total_in), 0).astype(BF16)
    outer_parts = masked(total_out)
    factor_in = factor(inner)
    factor_out = factor(jnp.concatenate(outer_parts, 0).astype(BF16))
    first_core = lax.axis_index("dp") % 2 == 0
    keep_ref[...] = jnp.where(first_core, factor_in, factor_out)
    send_ref[...] = jnp.where(first_core, factor_out, factor_in)
    signed = jnp.concatenate(
        [-part if s % 2 else part for s, part in enumerate(outer_parts)], 0
    ).astype(BF16)
    sketches = []
    for p in range(pairs):
        own_rows = slice(2 * p * seq, 2 * (p + 1) * seq)
        sketches.append(contract_first(signed[own_rows], inner[own_rows]))
    sketch_ref[...] = jnp.concatenate(sketches, 1)


def stage_kernel(*refs):
    count = len(refs) // 2
    arrived = refs[-1]
    copies = [
        pltpu.make_async_copy(refs[i], refs[count + i], arrived.at[i]) for i in range(count)
    ]
    for copy in copies:
        copy.start()
    for copy in copies:
        copy.wait()


def staged(*arrays):
    count = len(arrays)
    return pl.pallas_call(
        stage_kernel,
        out_shape=tuple(jax.ShapeDtypeStruct(a.shape, a.dtype) for a in arrays),
        in_specs=[whole(pl.ANY)] * count,
        out_specs=(whole(pl.ANY),) * count,
        scratch_shapes=[pltpu.SemaphoreType.DMA((count,))],
        compiler_params=params(1),
        cost_estimate=pl.CostEstimate(flops=0, bytes_accessed=2**22, transcendentals=0),
        name="stage",
    )(*arrays)


def gauss_jordan(tiles, width, group):
    count = len(tiles)
    sub = lax.broadcasted_iota(jnp.int32, tiles[0].shape, 0)
    shape = tiles[0].shape

    def spread_row(tile, j):
        return jnp.broadcast_to(tile[j : j + 1, :], shape)

    for start in range(0, width, group):
        columns = [
            [jnp.broadcast_to(tile[:, k : k + 1], shape) for tile in tiles]
            for k in range(start, start + group)
        ]
        for step in range(group):
            home, j = divmod(start + step, SUB)
            column = columns[step]
            inverse = 1.0 / spread_row(column[home], j)

            def eliminate(block):
                scaled = spread_row(block[home], j) * inverse
                result = [block[g] - column[g] * scaled for g in range(count)]
                result[home] = jnp.where(sub == j, scaled, result[home])
                return result

            for later in range(step + 1, group):
                columns[later] = eliminate(columns[later])
            tiles = eliminate(tiles)
    return tiles


def invert_kernel(blocks_ref, inverse_ref):
    rank = inverse_ref.shape[0]
    total = jnp.sum(blocks_ref[...], axis=0)
    slot, mirror, diagonal = packed_places(total.shape)

    def pick(mask):
        return jnp.sum(jnp.where(mask, total, 0.0), axis=(0, 1), keepdims=True)

    count = pick(slot)
    damp = 0.1 * (pick(diagonal) / count) / rank + 1e-06
    total = jnp.where(slot, pick(mirror), total)
    matrix = unpacked_symmetric(total / count + jnp.where(diagonal, damp, 0.0))
    row = lax.broadcasted_iota(jnp.int32, (rank, rank), 0)
    lane = lax.broadcasted_iota(jnp.int32, (rank, rank), 1)
    both = jnp.concatenate([matrix, jnp.where(row == lane, 1.0, 0.0)], 1)
    tiles = [both[g * SUB : (g + 1) * SUB] for g in range(rank // SUB)]
    tiles = gauss_jordan(tiles, rank, SUB)
    inverse_ref[...] = jnp.concatenate([tile[:, rank:] for tile in tiles], 0)


def exact_dot(a, b):
    return jnp.dot(a, b, precision=lax.Precision.HIGHEST, preferred_element_type=F32)


def score_kernel(
    bits, own_ref, other_ref, sketch_ref, *rest
):
    *evals_refs, scores_ref, rows_ref = rest
    place = lax.axis_index("dp")
    first_core = place % 2 == 0
    own = own_ref[...]
    other = other_ref[...]
    inverse_in = jnp.where(first_core, own, other)
    inverse_out = jnp.where(first_core, other, own)
    rank = own.shape[0]
    pairs, evals = scores_ref.shape
    left = exact_dot(inverse_out, sketch_ref[...])
    for p in range(pairs):
        rows_ref[p * rank : (p + 1) * rank, :] = exact_dot(
            left[:, p * rank : (p + 1) * rank], inverse_in
        )
    fold = 2 * LANES // rank
    steps = rank // fold
    precond = jnp.concatenate(
        [rows_ref[pl.ds(j, pairs * steps, stride=fold), :] for j in range(fold)], 1
    ).astype(BF16)
    row = lax.broadcasted_iota(jnp.int32, (pairs * steps, evals), 0) % steps
    total = jnp.zeros((pairs * steps, evals), F32)
    for g in range(steps):
        lanes = slice(g * fold * rank, (g + 1) * fold * rank)
        sketches = jnp.concatenate([ref[:, lanes] for ref in evals_refs], 0)
        total += jnp.where(row == g, contract_last(precond, sketches), 0.0)
    scores = jnp.concatenate(
        [jnp.sum(total[p * steps : (p + 1) * steps], 0, keepdims=True) for p in range(pairs)], 0
    )
    held = evals >> len(bits)
    column = lax.broadcasted_iota(jnp.int32, (evals, evals), 0)
    block = column // held
    source = jnp.full((evals, evals), place, jnp.int32)
    for i, bit in enumerate(bits):
        source = source ^ (((block >> i) & 1) * bit)
    target = source * held + column % held
    order = jnp.where(target == lax.broadcasted_iota(jnp.int32, (evals, evals), 1), 1.0, 0.0)
    scores_ref[...] = exact_dot(scores, order)


def params(mebibytes):
    return pltpu.CompilerParams(vmem_limit_bytes=mebibytes * 2**20)


def whole(space=VMEM):
    return pl.BlockSpec(memory_space=space)


def on_device(devices, activations, out_grads, lengths, proj_in, proj_out, eval_sketches):
    pairs, _, seq, depth = activations.shape
    rank = proj_in.shape[1]
    chips = devices // 2
    same_core = [[2 * chip + core for chip in range(chips)] for core in range(2)]
    bits = [2**i for i in range(2, devices.bit_length() - 1)] + [2, 1]
    first, *mid, late, _ = bits

    def swap(block, bit):
        return lax.ppermute(block, "dp", [(d, d ^ bit) for d in range(devices)])

    def copies_of(block):
        return jnp.broadcast_to(block[None], (chips,) + block.shape)

    def to_all_chips(copies):
        return lax.all_to_all(copies, "dp", 0, 0, axis_index_groups=same_core)

    def doubled(block, bit):
        return jnp.concatenate([block, swap(block, bit)], 0)

    rows = 2 * pairs * seq
    flat_in, flat_out, near = staged(
        activations.reshape(rows, depth), out_grads.reshape(rows, depth), eval_sketches
    )
    near = doubled(near, first)
    mine = jnp.concatenate([proj_in, proj_out], 1).T
    own = to_all_chips(copies_of(mine))
    own, near = lax.optimization_barrier((own, near))
    other = swap(own, 1)
    for bit in mid:
        near = doubled(near, bit)
    arriving = swap(near, late)
    evals_pieces = [near, arriving, swap(near, 1), swap(arriving, 1)]
    split_cores = mine.shape[1] % LANES == 0
    if not split_cores:
        first_core = lax.axis_index("dp") % 2 == 0
        stacked = jnp.where(
            first_core, jnp.stack([own, other], 1), jnp.stack([other, own], 1)
        )
        full = stacked.transpose(2, 0, 1, 3).reshape(2 * rank, depth)
        split = full.reshape(2 * rank, -1, 2, 2 * LANES).transpose(1, 2, 0, 3)
        own, other = split[:, 0], split[:, 1]

    def first_half(x, first):
        return pl.pallas_call(
            functools.partial(first_half_kernel, split_cores, first),
            out_shape=jax.ShapeDtypeStruct((rows, rank), F32),
            in_specs=[whole()] * 2,
            out_specs=whole(),
            compiler_params=params(8),
            cost_estimate=pl.CostEstimate(
                flops=rows * depth * rank, bytes_accessed=2 * rows * depth, transcendentals=0
            ),
            name="first_half",
        )(x, own)

    half_in = first_half(flat_in, 0)
    half_out = first_half(flat_out, rank)
    packed = jax.ShapeDtypeStruct((3 * rank // 8, 2 * rank), F32)
    keep, send, sketch = pl.pallas_call(
        functools.partial(second_half_kernel, split_cores),
        out_shape=(packed, packed, jax.ShapeDtypeStruct((rank, pairs * rank), F32)),
        in_specs=[whole(SMEM)] + [whole()] * 5,
        out_specs=(whole(),) * 3,
        compiler_params=params(8),
        cost_estimate=pl.CostEstimate(
            flops=2 * rows * depth * rank, bytes_accessed=4 * rows * depth, transcendentals=0
        ),
        name="second_half",
    )(lengths, flat_in, flat_out, other, half_in, half_out)
    sums = copies_of(keep + swap(send, 1))
    blocks = to_all_chips(sums)
    inverse = pl.pallas_call(
        invert_kernel,
        out_shape=jax.ShapeDtypeStruct((rank, rank), F32),
        in_specs=[whole()],
        out_specs=whole(),
        compiler_params=params(4),
        cost_estimate=pl.CostEstimate(flops=10**9, bytes_accessed=2**24, transcendentals=0),
        name="invert",
    )(blocks)
    other_inverse = swap(inverse, 1)
    evals = 4 * near.shape[0]
    return pl.pallas_call(
        functools.partial(score_kernel, bits),
        out_shape=jax.ShapeDtypeStruct((pairs, evals), F32),
        in_specs=[whole()] * 7,
        out_specs=whole(),
        scratch_shapes=[pltpu.VMEM((pairs * rank, rank), F32)],
        compiler_params=params(4 + 6 * evals * rank * rank // 2**20),
        name="score",
    )(inverse, other_inverse, sketch, *evals_pieces)


def solution(mesh):
    in_specs = (
        P(("groups", "dp"), None, None, None),
        P(("groups", "dp"), None, None, None),
        P(("groups", "dp"), None),
        P(("groups", "dp"), None),
        P(("groups", "dp"), None),
        P(("groups", "dp"), None),
    )
    out_specs = P(("groups", "dp"), None)
    return jax.shard_map(
        functools.partial(on_device, mesh.shape["dp"]),
        mesh=mesh,
        in_specs=in_specs,
        out_specs=out_specs,
        check_vma=False,
    )
```

```python
import functools

import jax
import jax.numpy as jnp
from jax import lax
from jax.experimental import pallas as pl
from jax.experimental.pallas import tpu as pltpu
from jax.sharding import PartitionSpec as P

F32 = jnp.float32
BF16 = jnp.bfloat16
LANES = 128
SUB = 8
VMEM = pltpu.VMEM
SMEM = pltpu.SMEM


def contract_last(a, b):
    return lax.dot_general(a, b, (((1,), (1,)), ((), ())), preferred_element_type=F32)


def contract_first(a, b):
    return lax.dot_general(a, b, (((0,), (0,)), ((), ())), preferred_element_type=F32)


def packed_symmetric(matrix):
    half = matrix.shape[0] // 2
    quarter = half // 4
    corners = (matrix[:half, :half], matrix[:half, half:], matrix[half:, half:])
    return jnp.concatenate(
        [
            jnp.concatenate([c[quarter * j : quarter * (j + 1)] for j in range(4)], 1)
            for c in corners
        ],
        0,
    )


def unpacked_symmetric(packed):
    quarter, wide = packed.shape[0] // 3, packed.shape[1]
    half = wide // 4
    corners = []
    for c in range(3):
        rows = packed[c * quarter : (c + 1) * quarter]
        corners.append(
            jnp.concatenate([rows[:, half * j : half * (j + 1)] for j in range(4)], 0)
        )
    first, cross, last = corners
    return jnp.concatenate(
        [jnp.concatenate([first, cross], 1), jnp.concatenate([cross.T, last], 1)], 0
    )


def packed_places(shape):
    quarter = shape[0] // 3
    half = shape[1] // 4
    row = lax.broadcasted_iota(jnp.int32, shape, 0)
    lane = lax.broadcasted_iota(jnp.int32, shape, 1)
    slot = (row == 0) & (lane == half)
    mirror = (row == 0) & (lane == quarter)
    diagonal = (lane % half == (lane // half) * quarter + row % quarter) & (
        (row < quarter) | (row >= 2 * quarter)
    )
    return slot, mirror, diagonal


def projected(x_ref, blocks_ref, first, rank, place, total):
    blocks, _, chunk = blocks_ref.shape
    for g in range(blocks):
        start = pl.multiple_of((2 * g + place) * chunk, chunk)
        total += contract_last(
            x_ref[:, pl.ds(start, chunk)], blocks_ref[g, first : first + rank, :]
        )
    return total


def own_place(split_cores):
    return lax.axis_index("dp") % 2 if split_cores else 0


def first_half_kernel(split_cores, first, x_ref, own_ref, total_ref):
    total_ref[...] = projected(
        x_ref,
        own_ref,
        first,
        total_ref.shape[1],
        own_place(split_cores),
        jnp.zeros(total_ref.shape, F32),
    )


def second_half_kernel(
    split_cores,
    live_ref,
    count_ref,
    act_ref,
    grad_ref,
    other_ref,
    half_in_ref,
    half_out_ref,
    keep_ref,
    send_ref,
    sketch_ref,
):
    place = 1 - own_place(split_cores)
    rows, rank = half_in_ref.shape
    pairs = sketch_ref.shape[1] // rank
    seq = rows // (2 * pairs)
    live = live_ref[...] > 0.0
    slot, _, _ = packed_places(keep_ref.shape)

    def factor(rows_of):
        packed = packed_symmetric(contract_first(rows_of, rows_of))
        return jnp.where(slot, count_ref[...], packed)

    total_in = projected(act_ref, other_ref, 0, rank, place, half_in_ref[...])
    total_out = projected(grad_ref, other_ref, rank, rank, place, half_out_ref[...])
    inner = jnp.where(live, total_in, 0.0).astype(BF16)
    outer = jnp.where(live, total_out, 0.0)
    factor_in = factor(inner)
    factor_out = factor(outer.astype(BF16))
    first_core = lax.axis_index("dp") % 2 == 0
    keep_ref[...] = jnp.where(first_core, factor_in, factor_out)
    send_ref[...] = jnp.where(first_core, factor_out, factor_in)
    signed = jnp.concatenate(
        [
            -outer[s * seq : (s + 1) * seq] if s % 2 else outer[s * seq : (s + 1) * seq]
            for s in range(2 * pairs)
        ],
        0,
    ).astype(BF16)
    sketches = []
    for p in range(pairs):
        own_rows = slice(2 * p * seq, 2 * (p + 1) * seq)
        sketches.append(contract_first(signed[own_rows], inner[own_rows]))
    sketch_ref[...] = jnp.concatenate(sketches, 1)


def stage_kernel(lengths_ref, *refs):
    *refs, live_ref, count_ref, arrived = refs
    count = len(refs) // 2
    copies = [
        pltpu.make_async_copy(refs[i], refs[count + i], arrived.at[i]) for i in range(count)
    ]
    for copy in copies:
        copy.start()
    pairs, responses = lengths_ref.shape
    seq = live_ref.shape[0] // (pairs * responses)
    token = lax.broadcasted_iota(jnp.int32, (seq, live_ref.shape[1]), 0)
    tokens = 0
    for s in range(pairs * responses):
        length = lengths_ref[s // responses, s % responses]
        live_ref[s * seq : (s + 1) * seq, :] = jnp.where(token < length, 1.0, 0.0)
        tokens += length
    count_ref[...] = jnp.full(count_ref.shape, tokens, jnp.int32).astype(F32)
    for copy in copies:
        copy.wait()


def staged(lengths, live, count, *arrays):
    return pl.pallas_call(
        stage_kernel,
        out_shape=tuple(jax.ShapeDtypeStruct(a.shape, a.dtype) for a in arrays)
        + (jax.ShapeDtypeStruct(live, F32), jax.ShapeDtypeStruct(count, F32)),
        in_specs=[whole(SMEM)] + [whole(pl.ANY)] * len(arrays),
        out_specs=(whole(pl.ANY),) * len(arrays) + (whole(), whole()),
        scratch_shapes=[pltpu.SemaphoreType.DMA((len(arrays),))],
        compiler_params=params(1),
        cost_estimate=pl.CostEstimate(flops=0, bytes_accessed=2**22, transcendentals=0),
        name="stage",
    )(lengths, *arrays)


def gauss_jordan(tiles, width, group):
    count = len(tiles)
    sub = lax.broadcasted_iota(jnp.int32, tiles[0].shape, 0)
    shape = tiles[0].shape

    def spread_row(tile, j):
        return jnp.broadcast_to(tile[j : j + 1, :], shape)

    for start in range(0, width, group):
        columns = [
            [jnp.broadcast_to(tile[:, k : k + 1], shape) for tile in tiles]
            for k in range(start, start + group)
        ]
        for step in range(group):
            home, j = divmod(start + step, SUB)
            column = columns[step]
            inverse = 1.0 / spread_row(column[home], j)

            def eliminate(block):
                scaled = spread_row(block[home], j) * inverse
                result = [block[g] - column[g] * scaled for g in range(count)]
                result[home] = jnp.where(sub == j, scaled, result[home])
                return result

            for later in range(step + 1, group):
                columns[later] = eliminate(columns[later])
            tiles = eliminate(tiles)
    return tiles


def invert_kernel(blocks_ref, inverse_ref):
    rank = inverse_ref.shape[0]
    total = jnp.sum(blocks_ref[...], axis=0)
    slot, mirror, diagonal = packed_places(total.shape)

    def pick(mask):
        return jnp.sum(jnp.where(mask, total, 0.0), axis=(0, 1), keepdims=True)

    count = pick(slot)
    damp = 0.1 * (pick(diagonal) / count) / rank + 1e-06
    total = jnp.where(slot, pick(mirror), total)
    matrix = unpacked_symmetric(total / count + jnp.where(diagonal, damp, 0.0))
    row = lax.broadcasted_iota(jnp.int32, (rank, rank), 0)
    lane = lax.broadcasted_iota(jnp.int32, (rank, rank), 1)
    both = jnp.concatenate([matrix, jnp.where(row == lane, 1.0, 0.0)], 1)
    tiles = [both[g * SUB : (g + 1) * SUB] for g in range(rank // SUB)]
    tiles = gauss_jordan(tiles, rank, SUB)
    inverse_ref[...] = jnp.concatenate([tile[:, rank:] for tile in tiles], 0)


def exact_dot(a, b):
    return jnp.dot(a, b, precision=lax.Precision.HIGHEST, preferred_element_type=F32)


def score_kernel(
    bits, own_ref, other_ref, sketch_ref, *rest
):
    *evals_refs, scores_ref, rows_ref = rest
    place = lax.axis_index("dp")
    first_core = place % 2 == 0
    own = own_ref[...]
    other = other_ref[...]
    inverse_in = jnp.where(first_core, own, other)
    inverse_out = jnp.where(first_core, other, own)
    rank = own.shape[0]
    pairs, evals = scores_ref.shape
    left = exact_dot(inverse_out, sketch_ref[...])
    for p in range(pairs):
        rows_ref[p * rank : (p + 1) * rank, :] = exact_dot(
            left[:, p * rank : (p + 1) * rank], inverse_in
        )
    fold = 2 * LANES // rank
    steps = rank // fold
    precond = jnp.concatenate(
        [rows_ref[pl.ds(j, pairs * steps, stride=fold), :] for j in range(fold)], 1
    ).astype(BF16)
    row = lax.broadcasted_iota(jnp.int32, (pairs * steps, evals), 0) % steps
    total = jnp.zeros((pairs * steps, evals), F32)
    for g in range(steps):
        lanes = slice(g * fold * rank, (g + 1) * fold * rank)
        sketches = jnp.concatenate([ref[:, lanes] for ref in evals_refs], 0)
        total += jnp.where(row == g, contract_last(precond, sketches), 0.0)
    scores = jnp.concatenate(
        [jnp.sum(total[p * steps : (p + 1) * steps], 0, keepdims=True) for p in range(pairs)], 0
    )
    held = evals >> len(bits)
    column = lax.broadcasted_iota(jnp.int32, (evals, evals), 0)
    block = column // held
    source = jnp.full((evals, evals), place, jnp.int32)
    for i, bit in enumerate(bits):
        source = source ^ (((block >> i) & 1) * bit)
    target = source * held + column % held
    order = jnp.where(target == lax.broadcasted_iota(jnp.int32, (evals, evals), 1), 1.0, 0.0)
    scores_ref[...] = exact_dot(scores, order)


def params(mebibytes):
    return pltpu.CompilerParams(vmem_limit_bytes=mebibytes * 2**20)


def whole(space=VMEM):
    return pl.BlockSpec(memory_space=space)


def on_device(devices, activations, out_grads, lengths, proj_in, proj_out, eval_sketches):
    pairs, _, seq, depth = activations.shape
    rank = proj_in.shape[1]
    chips = devices // 2
    same_core = [[2 * chip + core for chip in range(chips)] for core in range(2)]
    bits = [2**i for i in range(2, devices.bit_length() - 1)] + [2, 1]
    first, *mid, late, _ = bits

    def swap(block, bit):
        return lax.ppermute(block, "dp", [(d, d ^ bit) for d in range(devices)])

    def copies_of(block):
        return jnp.broadcast_to(block[None], (chips,) + block.shape)

    def to_all_chips(copies):
        return lax.all_to_all(copies, "dp", 0, 0, axis_index_groups=same_core)

    def doubled(block, bit):
        return jnp.concatenate([block, swap(block, bit)], 0)

    rows = 2 * pairs * seq
    packed = jax.ShapeDtypeStruct((3 * rank // 8, 2 * rank), F32)
    flat_in, flat_out, near, live, count = staged(
        lengths,
        (rows, rank),
        packed.shape,
        activations.reshape(rows, depth),
        out_grads.reshape(rows, depth),
        eval_sketches,
    )
    near = doubled(near, first)
    mine = jnp.concatenate([proj_in, proj_out], 1).T
    own = to_all_chips(copies_of(mine))
    own, near = lax.optimization_barrier((own, near))
    other = swap(own, 1)
    for bit in mid:
        near = doubled(near, bit)
    arriving = swap(near, late)
    evals_pieces = [near, arriving, swap(near, 1), swap(arriving, 1)]
    split_cores = mine.shape[1] % LANES == 0
    if not split_cores:
        first_core = lax.axis_index("dp") % 2 == 0
        stacked = jnp.where(
            first_core, jnp.stack([own, other], 1), jnp.stack([other, own], 1)
        )
        full = stacked.transpose(2, 0, 1, 3).reshape(2 * rank, depth)
        split = full.reshape(2 * rank, -1, 2, 2 * LANES).transpose(1, 2, 0, 3)
        own, other = split[:, 0], split[:, 1]

    def first_half(x, first):
        return pl.pallas_call(
            functools.partial(first_half_kernel, split_cores, first),
            out_shape=jax.ShapeDtypeStruct((rows, rank), F32),
            in_specs=[whole()] * 2,
            out_specs=whole(),
            compiler_params=params(8),
            cost_estimate=pl.CostEstimate(
                flops=rows * depth * rank, bytes_accessed=2 * rows * depth, transcendentals=0
            ),
            name="first_half",
        )(x, own)

    half_in = first_half(flat_in, 0)
    half_out = first_half(flat_out, rank)
    keep, send, sketch = pl.pallas_call(
        functools.partial(second_half_kernel, split_cores),
        out_shape=(packed, packed, jax.ShapeDtypeStruct((rank, pairs * rank), F32)),
        in_specs=[whole()] * 7,
        out_specs=(whole(),) * 3,
        compiler_params=params(8),
        cost_estimate=pl.CostEstimate(
            flops=2 * rows * depth * rank, bytes_accessed=4 * rows * depth, transcendentals=0
        ),
        name="second_half",
    )(live, count, flat_in, flat_out, other, half_in, half_out)
    sums = copies_of(keep + swap(send, 1))
    blocks = to_all_chips(sums)
    inverse = pl.pallas_call(
        invert_kernel,
        out_shape=jax.ShapeDtypeStruct((rank, rank), F32),
        in_specs=[whole()],
        out_specs=whole(),
        compiler_params=params(4),
        cost_estimate=pl.CostEstimate(flops=10**9, bytes_accessed=2**24, transcendentals=0),
        name="invert",
    )(blocks)
    other_inverse = swap(inverse, 1)
    evals = 4 * near.shape[0]
    return pl.pallas_call(
        functools.partial(score_kernel, bits),
        out_shape=jax.ShapeDtypeStruct((pairs, evals), F32),
        in_specs=[whole()] * 7,
        out_specs=whole(),
        scratch_shapes=[pltpu.VMEM((pairs * rank, rank), F32)],
        compiler_params=params(4 + 6 * evals * rank * rank // 2**20),
        name="score",
    )(inverse, other_inverse, sketch, *evals_pieces)


def solution(mesh):
    in_specs = (
        P(("groups", "dp"), None, None, None),
        P(("groups", "dp"), None, None, None),
        P(("groups", "dp"), None),
        P(("groups", "dp"), None),
        P(("groups", "dp"), None),
        P(("groups", "dp"), None),
    )
    out_specs = P(("groups", "dp"), None)
    return jax.shard_map(
        functools.partial(on_device, mesh.shape["dp"]),
        mesh=mesh,
        in_specs=in_specs,
        out_specs=out_specs,
        check_vma=False,
    )
```

```python
import functools

import jax
import jax.numpy as jnp
from jax import lax
from jax.experimental import pallas as pl
from jax.experimental.pallas import tpu as pltpu
from jax.sharding import PartitionSpec as P

F32 = jnp.float32
BF16 = jnp.bfloat16
LANES = 128
SUB = 8
VMEM = pltpu.VMEM
SMEM = pltpu.SMEM


def contract_last(a, b):
    return lax.dot_general(a, b, (((1,), (1,)), ((), ())), preferred_element_type=F32)


def contract_first(a, b):
    return lax.dot_general(a, b, (((0,), (0,)), ((), ())), preferred_element_type=F32)


def packed_symmetric(matrix):
    half = matrix.shape[0] // 2
    quarter = half // 4
    corners = (matrix[:half, :half], matrix[:half, half:], matrix[half:, half:])
    return jnp.concatenate(
        [
            jnp.concatenate([c[quarter * j : quarter * (j + 1)] for j in range(4)], 1)
            for c in corners
        ],
        0,
    )


def unpacked_symmetric(packed):
    quarter, wide = packed.shape[0] // 3, packed.shape[1]
    half = wide // 4
    corners = []
    for c in range(3):
        rows = packed[c * quarter : (c + 1) * quarter]
        corners.append(
            jnp.concatenate([rows[:, half * j : half * (j + 1)] for j in range(4)], 0)
        )
    first, cross, last = corners
    return jnp.concatenate(
        [jnp.concatenate([first, cross], 1), jnp.concatenate([cross.T, last], 1)], 0
    )


def packed_places(shape):
    quarter = shape[0] // 3
    half = shape[1] // 4
    row = lax.broadcasted_iota(jnp.int32, shape, 0)
    lane = lax.broadcasted_iota(jnp.int32, shape, 1)
    slot = (row == 0) & (lane == half)
    mirror = (row == 0) & (lane == quarter)
    diagonal = (lane % half == (lane // half) * quarter + row % quarter) & (
        (row < quarter) | (row >= 2 * quarter)
    )
    return slot, mirror, diagonal


def projected(x_ref, blocks_ref, first, rank, place, total):
    blocks, _, chunk = blocks_ref.shape
    for g in range(blocks):
        start = pl.multiple_of((2 * g + place) * chunk, chunk)
        total += contract_last(
            x_ref[:, pl.ds(start, chunk)], blocks_ref[g, first : first + rank, :]
        )
    return total


def own_place(split_cores):
    return lax.axis_index("dp") % 2 if split_cores else 0


def first_half_kernel(split_cores, first, x_ref, own_ref, total_ref):
    total_ref[...] = projected(
        x_ref,
        own_ref,
        first,
        total_ref.shape[1],
        own_place(split_cores),
        jnp.zeros(total_ref.shape, F32),
    )


def second_half_kernel(
    split_cores,
    live_ref,
    count_ref,
    act_ref,
    grad_ref,
    other_ref,
    half_in_ref,
    half_out_ref,
    keep_ref,
    send_ref,
    sketch_ref,
):
    place = 1 - own_place(split_cores)
    rows, rank = half_in_ref.shape
    pairs = sketch_ref.shape[1] // rank
    seq = rows // (2 * pairs)
    live = live_ref[...] > 0.0
    slot, _, _ = packed_places(keep_ref.shape)

    def factor(rows_of):
        packed = packed_symmetric(contract_first(rows_of, rows_of))
        return jnp.where(slot, count_ref[...], packed)

    total_in = projected(act_ref, other_ref, 0, rank, place, half_in_ref[...])
    total_out = projected(grad_ref, other_ref, rank, rank, place, half_out_ref[...])
    inner = jnp.where(live, total_in, 0.0).astype(BF16)
    outer = jnp.where(live, total_out, 0.0)
    factor_in = factor(inner)
    factor_out = factor(outer.astype(BF16))
    first_core = lax.axis_index("dp") % 2 == 0
    keep_ref[...] = jnp.where(first_core, factor_in, factor_out)
    send_ref[...] = jnp.where(first_core, factor_out, factor_in)
    signed = jnp.concatenate(
        [
            -outer[s * seq : (s + 1) * seq] if s % 2 else outer[s * seq : (s + 1) * seq]
            for s in range(2 * pairs)
        ],
        0,
    ).astype(BF16)
    sketches = []
    for p in range(pairs):
        own_rows = slice(2 * p * seq, 2 * (p + 1) * seq)
        sketches.append(contract_first(signed[own_rows], inner[own_rows]))
    sketch_ref[...] = jnp.concatenate(sketches, 1)


def stage_kernel(lengths_ref, evals_ref, *refs):
    *refs, live_ref, count_ref, same_evals_ref, arrived = refs
    count = len(refs) // 2
    copies = [
        pltpu.make_async_copy(refs[i], refs[count + i], arrived.at[i]) for i in range(count)
    ]
    for copy in copies:
        copy.start()
    pairs, responses = lengths_ref.shape
    seq = live_ref.shape[0] // (pairs * responses)
    token = lax.broadcasted_iota(jnp.int32, (seq, live_ref.shape[1]), 0)
    tokens = 0
    for s in range(pairs * responses):
        length = lengths_ref[s // responses, s % responses]
        live_ref[s * seq : (s + 1) * seq, :] = jnp.where(token < length, 1.0, 0.0)
        tokens += length
    same_evals_ref[...] = evals_ref[...]
    count_ref[...] = jnp.full(count_ref.shape, tokens, jnp.int32).astype(F32)
    for copy in copies:
        copy.wait()


def staged(lengths, evals, live, count, *arrays):
    return pl.pallas_call(
        stage_kernel,
        out_shape=tuple(jax.ShapeDtypeStruct(a.shape, a.dtype) for a in arrays)
        + (
            jax.ShapeDtypeStruct(live, F32),
            jax.ShapeDtypeStruct(count, F32),
            jax.ShapeDtypeStruct(evals.shape, evals.dtype),
        ),
        in_specs=[whole(SMEM), whole()] + [whole(pl.ANY)] * len(arrays),
        out_specs=(whole(pl.ANY),) * len(arrays) + (whole(),) * 3,
        scratch_shapes=[pltpu.SemaphoreType.DMA((len(arrays),))],
        compiler_params=params(1),
        cost_estimate=pl.CostEstimate(flops=0, bytes_accessed=2**22, transcendentals=0),
        name="stage",
    )(lengths, evals, *arrays)


def gauss_jordan(tiles, width, group):
    shape = tiles[0].shape
    sub = lax.broadcasted_iota(jnp.int32, shape, 0)

    def spread_row(tile, j):
        return jnp.broadcast_to(tile[j : j + 1, :], shape)

    def spread_column(tile, k):
        return jnp.broadcast_to(tile[:, k : k + 1], shape)

    for start in range(0, width, group):
        first, last = start // SUB, (start + group) // SUB
        pivots = [
            [spread_column(tile, k) for tile in tiles[first:last]]
            for k in range(start, start + group)
        ]
        rows = tiles[first:last]
        for step in range(group):
            home, j = divmod(step, SUB)
            column = pivots[step]
            inverse = 1.0 / spread_row(column[home], j)

            def eliminate(block):
                scaled = spread_row(block[home], j) * inverse
                result = [tile - c * scaled for tile, c in zip(block, column)]
                result[home] = jnp.where(sub == j, scaled, result[home])
                return result

            pivots[step + 1 :] = [eliminate(pivot) for pivot in pivots[step + 1 :]]
            rows = eliminate(rows)
        solved = [spread_row(rows[step // SUB], step % SUB) for step in range(group)]
        tiles = [
            rows[g - first]
            if first <= g < last
            else tile
            - functools.reduce(
                jnp.add, [spread_column(tile, start + t) * s for t, s in enumerate(solved)]
            )
            for g, tile in enumerate(tiles)
        ]
    return tiles


def invert_kernel(blocks_ref, inverse_ref):
    rank = inverse_ref.shape[0]
    total = jnp.sum(blocks_ref[...], axis=0)
    slot, mirror, diagonal = packed_places(total.shape)

    def pick(mask):
        return jnp.sum(jnp.where(mask, total, 0.0), axis=(0, 1), keepdims=True)

    count = pick(slot)
    damp = 0.1 * (pick(diagonal) / count) / rank + 1e-06
    total = jnp.where(slot, pick(mirror), total)
    matrix = unpacked_symmetric(total / count + jnp.where(diagonal, damp, 0.0))
    row = lax.broadcasted_iota(jnp.int32, (rank, rank), 0)
    lane = lax.broadcasted_iota(jnp.int32, (rank, rank), 1)
    both = jnp.concatenate([matrix, jnp.where(row == lane, 1.0, 0.0)], 1)
    tiles = [both[g * SUB : (g + 1) * SUB] for g in range(rank // SUB)]
    tiles = gauss_jordan(tiles, rank, 2 * SUB)
    inverse_ref[...] = jnp.concatenate([tile[:, rank:] for tile in tiles], 0)


def exact_dot(a, b):
    return jnp.dot(a, b, precision=lax.Precision.HIGHEST, preferred_element_type=F32)


def solve_kernel(inverse_ref, sketch_ref, left_ref):
    rank = inverse_ref.shape[0]
    first_core = lax.axis_index("dp") % 2 == 0

    @pl.when(first_core)
    def _():
        for p in range(0, sketch_ref.shape[1], rank):
            left_ref[:, p : p + rank] = exact_dot(sketch_ref[:, p : p + rank], inverse_ref[...])

    @pl.when(jnp.logical_not(first_core))
    def _():
        left_ref[...] = exact_dot(inverse_ref[...], sketch_ref[...])


def score_kernel(bits, other_ref, left_ref, *rest):
    *evals_refs, scores_ref, rows_ref = rest
    place = lax.axis_index("dp")
    first_core = place % 2 == 0
    rank = other_ref.shape[0]
    pairs, evals = scores_ref.shape

    @pl.when(first_core)
    def _():
        solved = exact_dot(other_ref[...], left_ref[...])
        for p in range(pairs):
            rows_ref[p * rank : (p + 1) * rank, :] = solved[:, p * rank : (p + 1) * rank]

    @pl.when(jnp.logical_not(first_core))
    def _():
        for p in range(pairs):
            rows_ref[p * rank : (p + 1) * rank, :] = exact_dot(
                left_ref[:, p * rank : (p + 1) * rank], other_ref[...]
            )

    fold = 2 * LANES // rank
    steps = rank // fold
    precond = jnp.concatenate(
        [rows_ref[pl.ds(j, pairs * steps, stride=fold), :] for j in range(fold)], 1
    ).astype(BF16)
    row = lax.broadcasted_iota(jnp.int32, (pairs * steps, evals), 0) % steps
    total = jnp.zeros((pairs * steps, evals), F32)
    for g in range(steps):
        lanes = slice(g * fold * rank, (g + 1) * fold * rank)
        sketches = jnp.concatenate([ref[:, lanes] for ref in evals_refs], 0)
        total += jnp.where(row == g, contract_last(precond, sketches), 0.0)
    scores = jnp.concatenate(
        [jnp.sum(total[p * steps : (p + 1) * steps], 0, keepdims=True) for p in range(pairs)], 0
    )
    held = evals >> len(bits)
    column = lax.broadcasted_iota(jnp.int32, (evals, evals), 0)
    block = column // held
    source = jnp.full((evals, evals), place, jnp.int32)
    for i, bit in enumerate(bits):
        source = source ^ (((block >> i) & 1) * bit)
    target = source * held + column % held
    order = jnp.where(target == lax.broadcasted_iota(jnp.int32, (evals, evals), 1), 1.0, 0.0)
    scores_ref[...] = exact_dot(scores, order)


def params(mebibytes):
    return pltpu.CompilerParams(vmem_limit_bytes=mebibytes * 2**20)


def whole(space=VMEM):
    return pl.BlockSpec(memory_space=space)


def on_device(devices, activations, out_grads, lengths, proj_in, proj_out, eval_sketches):
    pairs, _, seq, depth = activations.shape
    rank = proj_in.shape[1]
    chips = devices // 2
    same_core = [[2 * chip + core for chip in range(chips)] for core in range(2)]
    bits = [2**i for i in range(2, devices.bit_length() - 1)] + [2, 1]
    first, *mid, late, _ = bits

    def swap(block, bit):
        return lax.ppermute(block, "dp", [(d, d ^ bit) for d in range(devices)])

    def copies_of(block):
        return jnp.broadcast_to(block[None], (chips,) + block.shape)

    def to_all_chips(copies):
        return lax.all_to_all(copies, "dp", 0, 0, axis_index_groups=same_core)

    def doubled(block, bit):
        return jnp.concatenate([block, swap(block, bit)], 0)

    rows = 2 * pairs * seq
    packed = jax.ShapeDtypeStruct((3 * rank // 8, 2 * rank), F32)
    flat_in, flat_out, live, count, near = staged(
        lengths,
        eval_sketches,
        (rows, rank),
        packed.shape,
        activations.reshape(rows, depth),
        out_grads.reshape(rows, depth),
    )
    near = doubled(near, first)
    mine = jnp.concatenate([proj_in, proj_out], 1).T
    own = to_all_chips(copies_of(mine))
    own, near = lax.optimization_barrier((own, near))
    other = swap(own, 1)
    for bit in mid:
        near = doubled(near, bit)
    arriving = swap(near, late)
    evals_pieces = [near, arriving, swap(near, 1), swap(arriving, 1)]
    split_cores = mine.shape[1] % LANES == 0
    if not split_cores:
        first_core = lax.axis_index("dp") % 2 == 0
        stacked = jnp.where(
            first_core, jnp.stack([own, other], 1), jnp.stack([other, own], 1)
        )
        full = stacked.transpose(2, 0, 1, 3).reshape(2 * rank, depth)
        split = full.reshape(2 * rank, -1, 2, 2 * LANES).transpose(1, 2, 0, 3)
        own, other = split[:, 0], split[:, 1]

    def first_half(x, first):
        return pl.pallas_call(
            functools.partial(first_half_kernel, split_cores, first),
            out_shape=jax.ShapeDtypeStruct((rows, rank), F32),
            in_specs=[whole()] * 2,
            out_specs=whole(),
            compiler_params=params(8),
            cost_estimate=pl.CostEstimate(
                flops=rows * depth * rank, bytes_accessed=2 * rows * depth, transcendentals=0
            ),
            name="first_half",
        )(x, own)

    half_in = first_half(flat_in, 0)
    half_out = first_half(flat_out, rank)
    keep, send, sketch = pl.pallas_call(
        functools.partial(second_half_kernel, split_cores),
        out_shape=(packed, packed, jax.ShapeDtypeStruct((rank, pairs * rank), F32)),
        in_specs=[whole()] * 7,
        out_specs=(whole(),) * 3,
        compiler_params=params(8),
        cost_estimate=pl.CostEstimate(
            flops=2 * rows * depth * rank, bytes_accessed=4 * rows * depth, transcendentals=0
        ),
        name="second_half",
    )(live, count, flat_in, flat_out, other, half_in, half_out)
    sums = copies_of(keep + swap(send, 1))
    blocks = to_all_chips(sums)
    inverse = pl.pallas_call(
        invert_kernel,
        out_shape=jax.ShapeDtypeStruct((rank, rank), F32),
        in_specs=[whole()],
        out_specs=whole(),
        compiler_params=params(4),
        cost_estimate=pl.CostEstimate(flops=10**9, bytes_accessed=2**24, transcendentals=0),
        name="invert",
    )(blocks)
    other_inverse = swap(inverse, 1)
    left = pl.pallas_call(
        solve_kernel,
        out_shape=jax.ShapeDtypeStruct((rank, pairs * rank), F32),
        in_specs=[whole()] * 2,
        out_specs=whole(),
        compiler_params=params(4),
        cost_estimate=pl.CostEstimate(flops=10**8, bytes_accessed=2**21, transcendentals=0),
        name="solve",
    )(inverse, sketch)
    evals = 4 * near.shape[0]
    return pl.pallas_call(
        functools.partial(score_kernel, bits),
        out_shape=jax.ShapeDtypeStruct((pairs, evals), F32),
        in_specs=[whole()] * 6,
        out_specs=whole(),
        scratch_shapes=[pltpu.VMEM((pairs * rank, rank), F32)],
        compiler_params=params(4 + 6 * evals * rank * rank // 2**20),
        name="score",
    )(other_inverse, left, *evals_pieces)


def solution(mesh):
    in_specs = (
        P(("groups", "dp"), None, None, None),
        P(("groups", "dp"), None, None, None),
        P(("groups", "dp"), None),
        P(("groups", "dp"), None),
        P(("groups", "dp"), None),
        P(("groups", "dp"), None),
    )
    out_specs = P(("groups", "dp"), None)
    return jax.shard_map(
        functools.partial(on_device, mesh.shape["dp"]),
        mesh=mesh,
        in_specs=in_specs,
        out_specs=out_specs,
        check_vma=False,
    )
```

```python
import functools

import jax
import jax.numpy as jnp
from jax import lax
from jax.experimental import pallas as pl
from jax.experimental.pallas import tpu as pltpu
from jax.sharding import PartitionSpec as P

F32 = jnp.float32
BF16 = jnp.bfloat16
LANES = 128
SUB = 8
VMEM = pltpu.VMEM
SMEM = pltpu.SMEM


def contract_last(a, b):
    return lax.dot_general(a, b, (((1,), (1,)), ((), ())), preferred_element_type=F32)


def contract_first(a, b):
    return lax.dot_general(a, b, (((0,), (0,)), ((), ())), preferred_element_type=F32)


def packed_symmetric(matrix):
    half = matrix.shape[0] // 2
    quarter = half // 4
    corners = (matrix[:half, :half], matrix[:half, half:], matrix[half:, half:])
    return jnp.concatenate(
        [
            jnp.concatenate([c[quarter * j : quarter * (j + 1)] for j in range(4)], 1)
            for c in corners
        ],
        0,
    )


def unpacked_symmetric(packed):
    quarter, wide = packed.shape[0] // 3, packed.shape[1]
    half = wide // 4
    corners = []
    for c in range(3):
        rows = packed[c * quarter : (c + 1) * quarter]
        corners.append(
            jnp.concatenate([rows[:, half * j : half * (j + 1)] for j in range(4)], 0)
        )
    first, cross, last = corners
    return jnp.concatenate(
        [jnp.concatenate([first, cross], 1), jnp.concatenate([cross.T, last], 1)], 0
    )


def packed_places(shape):
    quarter = shape[0] // 3
    half = shape[1] // 4
    row = lax.broadcasted_iota(jnp.int32, shape, 0)
    lane = lax.broadcasted_iota(jnp.int32, shape, 1)
    slot = (row == 0) & (lane == half)
    mirror = (row == 0) & (lane == quarter)
    diagonal = (lane % half == (lane // half) * quarter + row % quarter) & (
        (row < quarter) | (row >= 2 * quarter)
    )
    return slot, mirror, diagonal


def projected(x_ref, blocks_ref, first, rank, place, total):
    blocks, _, chunk = blocks_ref.shape
    for g in range(blocks):
        start = pl.multiple_of((2 * g + place) * chunk, chunk)
        total += contract_last(
            x_ref[:, pl.ds(start, chunk)], blocks_ref[g, first : first + rank, :]
        )
    return total


def own_place(split_cores):
    return lax.axis_index("dp") % 2 if split_cores else 0


def first_half_kernel(split_cores, first, x_ref, own_ref, total_ref):
    total_ref[...] = projected(
        x_ref,
        own_ref,
        first,
        total_ref.shape[1],
        own_place(split_cores),
        jnp.zeros(total_ref.shape, F32),
    )


def second_half_kernel(
    split_cores,
    outer_core,
    live_ref,
    count_ref,
    act_ref,
    grad_ref,
    other_ref,
    half_in_ref,
    half_out_ref,
    factor_ref,
    tokens_ref,
):
    place = 1 - own_place(split_cores)
    rank = half_in_ref.shape[1]
    slot, _, _ = packed_places(factor_ref.shape)

    def side(x_ref, first, half_ref):
        total = projected(x_ref, other_ref, first, rank, place, half_ref[...])
        tokens = jnp.where(live_ref[...] > 0.0, total, 0.0).astype(BF16)
        packed = packed_symmetric(contract_first(tokens, tokens))
        factor_ref[...] = jnp.where(slot, count_ref[...], packed)
        tokens_ref[...] = tokens

    outer_here = lax.axis_index("dp") % 2 == outer_core

    @pl.when(outer_here)
    def _():
        side(grad_ref, rank, half_out_ref)

    @pl.when(jnp.logical_not(outer_here))
    def _():
        side(act_ref, 0, half_in_ref)


def sketch_kernel(sent_ref, kept_ref, sketch_ref):
    rank = sent_ref.shape[1]
    pairs = sketch_ref.shape[1] // rank
    seq = sent_ref.shape[0] // (2 * pairs)

    def sketch(outer_ref, inner_ref):
        for p in range(pairs):
            start = 2 * p * seq
            chosen = slice(start, start + seq)
            rejected = slice(start + seq, start + 2 * seq)
            signed = jnp.concatenate([outer_ref[chosen, :], -outer_ref[rejected, :]], 0)
            sketch_ref[:, p * rank : (p + 1) * rank] = contract_first(
                signed, inner_ref[start : start + 2 * seq, :]
            )

    first_core = lax.axis_index("dp") % 2 == 0

    @pl.when(first_core)
    def _():
        sketch(sent_ref, kept_ref)

    @pl.when(jnp.logical_not(first_core))
    def _():
        sketch(kept_ref, sent_ref)


def stage_kernel(lengths_ref, evals_ref, *refs):
    *refs, live_ref, count_ref, same_evals_ref, arrived = refs
    count = len(refs) // 2
    copies = [
        pltpu.make_async_copy(refs[i], refs[count + i], arrived.at[i]) for i in range(count)
    ]
    for copy in copies:
        copy.start()
    pairs, responses = lengths_ref.shape
    seq = live_ref.shape[0] // (pairs * responses)
    token = lax.broadcasted_iota(jnp.int32, (seq, live_ref.shape[1]), 0)
    tokens = 0
    for s in range(pairs * responses):
        length = lengths_ref[s // responses, s % responses]
        live_ref[s * seq : (s + 1) * seq, :] = jnp.where(token < length, 1.0, 0.0)
        tokens += length
    same_evals_ref[...] = evals_ref[...]
    count_ref[...] = jnp.full(count_ref.shape, tokens, jnp.int32).astype(F32)
    for copy in copies:
        copy.wait()


def staged(lengths, evals, live, count, *arrays):
    return pl.pallas_call(
        stage_kernel,
        out_shape=tuple(jax.ShapeDtypeStruct(a.shape, a.dtype) for a in arrays)
        + (
            jax.ShapeDtypeStruct(live, F32),
            jax.ShapeDtypeStruct(count, F32),
            jax.ShapeDtypeStruct(evals.shape, evals.dtype),
        ),
        in_specs=[whole(SMEM), whole()] + [whole(pl.ANY)] * len(arrays),
        out_specs=(whole(pl.ANY),) * len(arrays) + (whole(),) * 3,
        scratch_shapes=[pltpu.SemaphoreType.DMA((len(arrays),))],
        compiler_params=params(1),
        cost_estimate=pl.CostEstimate(flops=0, bytes_accessed=2**22, transcendentals=0),
        name="stage",
    )(lengths, evals, *arrays)


def gauss_jordan(tiles, width, group):
    shape = tiles[0].shape
    sub = lax.broadcasted_iota(jnp.int32, shape, 0)

    def spread_row(tile, j):
        return jnp.broadcast_to(tile[j : j + 1, :], shape)

    def spread_column(tile, k):
        return jnp.broadcast_to(tile[:, k : k + 1], shape)

    for start in range(0, width, group):
        first, last = start // SUB, (start + group) // SUB
        pivots = [
            [spread_column(tile, k) for tile in tiles[first:last]]
            for k in range(start, start + group)
        ]
        rows = tiles[first:last]
        for step in range(group):
            home, j = divmod(step, SUB)
            column = pivots[step]
            inverse = 1.0 / spread_row(column[home], j)

            def eliminate(block):
                scaled = spread_row(block[home], j) * inverse
                result = [tile - c * scaled for tile, c in zip(block, column)]
                result[home] = jnp.where(sub == j, scaled, result[home])
                return result

            pivots[step + 1 :] = [eliminate(pivot) for pivot in pivots[step + 1 :]]
            rows = eliminate(rows)
        solved = [spread_row(rows[step // SUB], step % SUB) for step in range(group)]
        tiles = [
            rows[g - first]
            if first <= g < last
            else tile
            - functools.reduce(
                jnp.add, [spread_column(tile, start + t) * s for t, s in enumerate(solved)]
            )
            for g, tile in enumerate(tiles)
        ]
    return tiles


def invert_kernel(blocks_ref, inverse_ref):
    rank = inverse_ref.shape[0]
    total = jnp.sum(blocks_ref[...], axis=0)
    slot, mirror, diagonal = packed_places(total.shape)

    def pick(mask):
        return jnp.sum(jnp.where(mask, total, 0.0), axis=(0, 1), keepdims=True)

    count = pick(slot)
    damp = 0.1 * (pick(diagonal) / count) / rank + 1e-06
    total = jnp.where(slot, pick(mirror), total)
    matrix = unpacked_symmetric(total / count + jnp.where(diagonal, damp, 0.0))
    row = lax.broadcasted_iota(jnp.int32, (rank, rank), 0)
    lane = lax.broadcasted_iota(jnp.int32, (rank, rank), 1)
    both = jnp.concatenate([matrix, jnp.where(row == lane, 1.0, 0.0)], 1)
    tiles = [both[g * SUB : (g + 1) * SUB] for g in range(rank // SUB)]
    tiles = gauss_jordan(tiles, rank, 2 * SUB)
    inverse_ref[...] = jnp.concatenate([tile[:, rank:] for tile in tiles], 0)


def exact_dot(a, b):
    return jnp.dot(a, b, precision=lax.Precision.HIGHEST, preferred_element_type=F32)


def solve_kernel(inverse_ref, sketch_ref, left_ref):
    rank = inverse_ref.shape[0]
    first_core = lax.axis_index("dp") % 2 == 0

    @pl.when(first_core)
    def _():
        for p in range(0, sketch_ref.shape[1], rank):
            left_ref[:, p : p + rank] = exact_dot(sketch_ref[:, p : p + rank], inverse_ref[...])

    @pl.when(jnp.logical_not(first_core))
    def _():
        left_ref[...] = exact_dot(inverse_ref[...], sketch_ref[...])


def score_kernel(bits, other_ref, left_ref, *rest):
    *evals_refs, scores_ref, rows_ref = rest
    place = lax.axis_index("dp")
    first_core = place % 2 == 0
    rank = other_ref.shape[0]
    pairs, evals = scores_ref.shape

    @pl.when(first_core)
    def _():
        solved = exact_dot(other_ref[...], left_ref[...])
        for p in range(pairs):
            rows_ref[p * rank : (p + 1) * rank, :] = solved[:, p * rank : (p + 1) * rank]

    @pl.when(jnp.logical_not(first_core))
    def _():
        for p in range(pairs):
            rows_ref[p * rank : (p + 1) * rank, :] = exact_dot(
                left_ref[:, p * rank : (p + 1) * rank], other_ref[...]
            )

    fold = 2 * LANES // rank
    steps = rank // fold
    precond = jnp.concatenate(
        [rows_ref[pl.ds(j, pairs * steps, stride=fold), :] for j in range(fold)], 1
    ).astype(BF16)
    row = lax.broadcasted_iota(jnp.int32, (pairs * steps, evals), 0) % steps
    total = jnp.zeros((pairs * steps, evals), F32)
    for g in range(steps):
        lanes = slice(g * fold * rank, (g + 1) * fold * rank)
        sketches = jnp.concatenate([ref[:, lanes] for ref in evals_refs], 0)
        total += jnp.where(row == g, contract_last(precond, sketches), 0.0)
    scores = jnp.concatenate(
        [jnp.sum(total[p * steps : (p + 1) * steps], 0, keepdims=True) for p in range(pairs)], 0
    )
    held = evals >> len(bits)
    column = lax.broadcasted_iota(jnp.int32, (evals, evals), 0)
    block = column // held
    source = jnp.full((evals, evals), place, jnp.int32)
    for i, bit in enumerate(bits):
        source = source ^ (((block >> i) & 1) * bit)
    target = source * held + column % held
    order = jnp.where(target == lax.broadcasted_iota(jnp.int32, (evals, evals), 1), 1.0, 0.0)
    scores_ref[...] = exact_dot(scores, order)


def params(mebibytes):
    return pltpu.CompilerParams(vmem_limit_bytes=mebibytes * 2**20)


def whole(space=VMEM):
    return pl.BlockSpec(memory_space=space)


def on_device(devices, activations, out_grads, lengths, proj_in, proj_out, eval_sketches):
    pairs, _, seq, depth = activations.shape
    rank = proj_in.shape[1]
    chips = devices // 2
    same_core = [[2 * chip + core for chip in range(chips)] for core in range(2)]
    bits = [2**i for i in range(2, devices.bit_length() - 1)] + [2, 1]
    first, *mid, late, _ = bits

    def swap(block, bit):
        return lax.ppermute(block, "dp", [(d, d ^ bit) for d in range(devices)])

    def copies_of(block):
        return jnp.broadcast_to(block[None], (chips,) + block.shape)

    def to_all_chips(copies):
        return lax.all_to_all(copies, "dp", 0, 0, axis_index_groups=same_core)

    def doubled(block, bit):
        return jnp.concatenate([block, swap(block, bit)], 0)

    rows = 2 * pairs * seq
    packed = jax.ShapeDtypeStruct((3 * rank // 8, 2 * rank), F32)
    flat_in, flat_out, live, count, near = staged(
        lengths,
        eval_sketches,
        (rows, rank),
        packed.shape,
        activations.reshape(rows, depth),
        out_grads.reshape(rows, depth),
    )
    near = doubled(near, first)
    mine = jnp.concatenate([proj_in, proj_out], 1).T
    own = to_all_chips(copies_of(mine))
    own, near = lax.optimization_barrier((own, near))
    other = swap(own, 1)
    for bit in mid:
        near = doubled(near, bit)
    arriving = swap(near, late)
    evals_pieces = [near, arriving, swap(near, 1), swap(arriving, 1)]
    split_cores = mine.shape[1] % LANES == 0
    if not split_cores:
        first_core = lax.axis_index("dp") % 2 == 0
        stacked = jnp.where(
            first_core, jnp.stack([own, other], 1), jnp.stack([other, own], 1)
        )
        full = stacked.transpose(2, 0, 1, 3).reshape(2 * rank, depth)
        split = full.reshape(2 * rank, -1, 2, 2 * LANES).transpose(1, 2, 0, 3)
        own, other = split[:, 0], split[:, 1]

    def first_half(x, first):
        return pl.pallas_call(
            functools.partial(first_half_kernel, split_cores, first),
            out_shape=jax.ShapeDtypeStruct((rows, rank), F32),
            in_specs=[whole()] * 2,
            out_specs=whole(),
            compiler_params=params(8),
            cost_estimate=pl.CostEstimate(
                flops=rows * depth * rank, bytes_accessed=2 * rows * depth, transcendentals=0
            ),
            name="first_half",
        )(x, own)

    half_in = first_half(flat_in, 0)
    half_out = first_half(flat_out, rank)
    def second_half(outer_core):
        return pl.pallas_call(
            functools.partial(second_half_kernel, split_cores, outer_core),
            out_shape=(packed, jax.ShapeDtypeStruct((rows, rank), BF16)),
            in_specs=[whole()] * 7,
            out_specs=(whole(),) * 2,
            compiler_params=params(8),
            cost_estimate=pl.CostEstimate(
                flops=rows * depth * rank, bytes_accessed=2 * rows * depth, transcendentals=0
            ),
            name="second_half",
        )(live, count, flat_in, flat_out, other, half_in, half_out)

    send, sent = second_half(0)
    arrived = swap(send, 1)
    keep, kept = second_half(1)
    sketch = pl.pallas_call(
        sketch_kernel,
        out_shape=jax.ShapeDtypeStruct((rank, pairs * rank), F32),
        in_specs=[whole()] * 2,
        out_specs=whole(),
        compiler_params=params(4),
        cost_estimate=pl.CostEstimate(flops=10**8, bytes_accessed=2**21, transcendentals=0),
        name="sketch",
    )(sent, kept)
    sums = copies_of(keep + arrived)
    blocks = to_all_chips(sums)
    inverse = pl.pallas_call(
        invert_kernel,
        out_shape=jax.ShapeDtypeStruct((rank, rank), F32),
        in_specs=[whole()],
        out_specs=whole(),
        compiler_params=params(4),
        cost_estimate=pl.CostEstimate(flops=10**9, bytes_accessed=2**24, transcendentals=0),
        name="invert",
    )(blocks)
    other_inverse = swap(inverse, 1)
    left = pl.pallas_call(
        solve_kernel,
        out_shape=jax.ShapeDtypeStruct((rank, pairs * rank), F32),
        in_specs=[whole()] * 2,
        out_specs=whole(),
        compiler_params=params(4),
        cost_estimate=pl.CostEstimate(flops=10**8, bytes_accessed=2**21, transcendentals=0),
        name="solve",
    )(inverse, sketch)
    evals = 4 * near.shape[0]
    return pl.pallas_call(
        functools.partial(score_kernel, bits),
        out_shape=jax.ShapeDtypeStruct((pairs, evals), F32),
        in_specs=[whole()] * 6,
        out_specs=whole(),
        scratch_shapes=[pltpu.VMEM((pairs * rank, rank), F32)],
        compiler_params=params(4 + 6 * evals * rank * rank // 2**20),
        name="score",
    )(other_inverse, left, *evals_pieces)


def solution(mesh):
    in_specs = (
        P(("groups", "dp"), None, None, None),
        P(("groups", "dp"), None, None, None),
        P(("groups", "dp"), None),
        P(("groups", "dp"), None),
        P(("groups", "dp"), None),
        P(("groups", "dp"), None),
    )
    out_specs = P(("groups", "dp"), None)
    return jax.shard_map(
        functools.partial(on_device, mesh.shape["dp"]),
        mesh=mesh,
        in_specs=in_specs,
        out_specs=out_specs,
        check_vma=False,
    )
```
